32 devices in a mesh: lat: 4 (over x, core), lon: 8 (over z, y).
Axes of the slice: x: 2, y: 2, z: 4, core: 2. Of those that a mesh axis runs over, the one named last changes fastest.
Arguments:
- atm_fluxes: bfloat16 [24, 65536], P(None, ('lat', 'lon')), may hold values from -6 to 6
- remap_weights: bfloat16 [32, 64, 128, 128], P(('lat', 'lon')), may hold values from 0 to 0.015625
- source_block: int32 [32, 64], P(('lat', 'lon')), may hold values from 0 to 15
- target_block: int32 [32, 64], P(('lat', 'lon')), may hold values from 0 to 15
- block_count: int32 [32, 32], P(('lat', 'lon')), may hold values from 1 to 2, as said below
- tracers: float32 [6, 16, 64, 1024], P(None, None, 'lat', 'lon'), may hold values from -6 to 6
- east_velocity: float32 [16, 64, 1024], P(None, 'lat', 'lon'), may hold values from -0.3 to 0.3
- north_velocity: float32 [16, 64, 1024], P(None, 'lat', 'lon'), may hold values from -0.3 to 0.3
- land_mask: int32 [64, 1024], P('lat', 'lon'), may hold values 0 or 1
- coupling: float32 [96, 24], replicated, may hold values from -3 to 3
Outputs:
- tracer_out: float32 [6, 16, 64, 1024], P(None, None, 'lat', 'lon')
The draws below stay inside these ranges and needn't reach their ends.
Inputs may be any that keep to these rules, and one draw needn't show every extreme that they name: Slots 0 to block_count - 1 of a source and tile carry data; in every draw one tile receives all 2 slots from every source.
All inputs are finite; a program needn't handle non-finite values. No bound on the sum of `land_mask` on one device may be relied on, other than what follows from the above.
Results may differ from the reference program's by a relative error of at most 0.0003.
Values sent between devices are 32-bit elements; how exact they have to be, the bound alone decides.
A program may use at most 128 MiB of HBM per device.

```python
import jax
import jax.numpy as jnp
from jax import lax

NFLX = 24
NTR = 6
BLOCK = 128
LEV = 16
NSUB = 4
SLOTS = 2
CLAT = 16
ABLK = 16
TILES = 32
NLAT = 64
NLON = 1024
ACELLS = 65536
N_LAT = 4
N_LON = 8


def draw_block_count(key, part):
    base_key = jax.random.fold_in(key, 11)
    full_key = jax.random.fold_in(key, 23)
    base = jax.random.randint(base_key, (TILES, TILES), 1, SLOTS + 1, dtype=jnp.int32)
    full_tile = jax.random.randint(full_key, (), 0, TILES, dtype=jnp.int32)
    columns = jnp.arange(TILES, dtype=jnp.int32)[None, :]
    return jnp.where(columns == full_tile, jnp.int32(SLOTS), base)


def touch_ends(entries, key, least, top_value):
    dims = entries.shape
    spot = [jax.random.randint(jax.random.fold_in(key, axis), (), 0, dims[axis]) for axis in range(len(dims))]
    entries = entries.at[tuple(spot)].set(least)
    longest = dims.index(max(dims))
    spot[longest] = (spot[longest] + 1) % dims[longest]
    return entries.at[tuple(spot)].set(top_value)


def steps_of(own_key, dims, cuts, low, top_value):
    level = 1.0
    for axis_at, blocks in cuts:
        heights = jax.random.uniform(jax.random.fold_in(jax.random.fold_in(own_key, 6), axis_at), (blocks,), jnp.float32, low / len(cuts), top_value / len(cuts))
        level = level * jnp.repeat(jnp.exp(heights), dims[axis_at] // blocks).reshape((-1,) + (1,) * (len(dims) - 1 - axis_at))
    return level


def centred(stream_key, dims, deviation, limit, pieces=(), kind=jnp.bfloat16):
    drawn = jax.random.normal(stream_key, dims, jnp.float32) * deviation
    if len(pieces) > 0:
        drawn = steps_of(stream_key, dims, pieces, -0.22, 0.18) * drawn
    return jnp.clip(drawn, min=-limit, max=limit).astype(kind)


def setup_inputs(seed: int = 0) -> dict:
    key_of = jax.random.split(jax.random.key(seed), 11)
    atm_fluxes = centred(key_of[0], (NFLX, ACELLS), 1.0, 6.0, ((1, 32),))
    remap_weights = jnp.clip(0.015625 * jax.random.uniform(key_of[1], (TILES, TILES * SLOTS, BLOCK, BLOCK), jnp.float32) ** steps_of(key_of[1], (TILES, TILES * SLOTS, BLOCK, BLOCK), ((0, 32),), -0.2, 0.2), 0.0, 0.015625).astype(jnp.bfloat16)
    source_block = touch_ends(jax.random.randint(key_of[2], (TILES, TILES * SLOTS), 0, ABLK), jax.random.fold_in(key_of[2], 1), 0, ABLK - 1).astype(jnp.int32)
    target_block = touch_ends(jax.random.randint(key_of[3], (TILES, TILES * SLOTS), 0, CLAT), jax.random.fold_in(key_of[3], 1), 0, CLAT - 1).astype(jnp.int32)
    block_count = draw_block_count(jax.random.fold_in(key_of[10], 71), 0)
    tracers = centred(key_of[5], (NTR, LEV, NLAT, NLON), 1.0, 6.0, ((2, 4), (3, 8)), jnp.float32)
    east_velocity = jnp.clip(jax.random.uniform(key_of[6], (LEV, NLAT, NLON), jnp.float32, -0.3, 0.3) * steps_of(key_of[6], (LEV, NLAT, NLON), ((1, 4), (2, 8)), -0.4, 0.0), -0.3, 0.3)
    north_velocity = jnp.clip(jax.random.uniform(key_of[7], (LEV, NLAT, NLON), jnp.float32, -0.3, 0.3) * steps_of(key_of[7], (LEV, NLAT, NLON), ((1, 4), (2, 8)), -0.4, 0.0), -0.3, 0.3)
    land_mask = touch_ends((jax.random.randint(key_of[8], (NLAT, NLON), 0, 10) < 7).astype(jnp.int32), jax.random.fold_in(key_of[8], 1), 0, 1)
    coupling = centred(key_of[9], (NTR * LEV, NFLX), 0.5, 3.0, (), jnp.float32)
    return {"atm_fluxes": atm_fluxes, "remap_weights": remap_weights, "source_block": source_block, "target_block": target_block, "block_count": block_count, "tracers": tracers, "east_velocity": east_velocity, "north_velocity": north_velocity, "land_mask": land_mask, "coupling": coupling}


diffusion_number = 0.2


def advect(tracer_now, east_speed, north_speed, sea_mask):
    mask_east = sea_mask[:, :-1] * sea_mask[:, 1:]
    east_flow = mask_east * (east_speed[:, :, :-1] * (tracer_now[..., :-1] + tracer_now[..., 1:]) * 0.5 - diffusion_number * (tracer_now[..., 1:] - tracer_now[..., :-1]))
    mask_north = sea_mask[:-1, :] * sea_mask[1:, :]
    north_flow = mask_north * (north_speed[:, :-1, :] * (tracer_now[..., :-1, :] + tracer_now[..., 1:, :]) * 0.5 - diffusion_number * (tracer_now[..., 1:, :] - tracer_now[..., :-1, :]))
    inner = tracer_now[..., 1:-1, 1:-1]
    return inner + east_flow[..., 1:-1, :-1] - east_flow[..., 1:-1, 1:] + north_flow[..., :-1, 1:-1] - north_flow[..., 1:, 1:-1]


def extend(field):
    widths = [(0, 0)] * (field.ndim - 2) + [(1, 1), (0, 0)]
    padded = jnp.pad(field, widths)
    return jnp.concatenate([padded[..., -1:], padded, padded[..., :1]], axis=-1)


def reference(atm_fluxes, remap_weights, source_block, target_block, block_count, tracers, east_velocity, north_velocity, land_mask, coupling):
    atm_blocks = atm_fluxes.astype(jnp.float32).reshape(NFLX, TILES, ABLK, BLOCK)
    slot_ids = jnp.arange(TILES * SLOTS, dtype=jnp.int32)
    dest_tile = slot_ids // SLOTS
    is_live = (slot_ids % SLOTS)[None, :] < jnp.repeat(block_count, SLOTS, axis=1)

    def add_source(source_dev, totals):
        local = lax.dynamic_index_in_dim(atm_blocks, source_dev, 1, keepdims=False)
        chosen = jnp.take(local, source_block[source_dev], axis=1)
        weights = remap_weights[source_dev].astype(jnp.float32)
        partial_value = jnp.einsum("fsb,sbc->sfc", chosen, weights, precision=lax.Precision.HIGHEST)
        partial_value = jnp.where(is_live[source_dev][:, None, None], partial_value, jnp.float32(0.0))
        return totals.at[dest_tile, target_block[source_dev]].add(partial_value)

    totals = lax.fori_loop(0, TILES, add_source, jnp.zeros((TILES, CLAT, NFLX, BLOCK), jnp.float32))
    ocean_flux = totals.reshape(N_LAT, N_LON, CLAT, NFLX, BLOCK).transpose(3, 0, 2, 1, 4).reshape(NFLX, NLAT, NLON)
    source = jnp.einsum("pf,fij->pij", coupling, ocean_flux, precision=lax.Precision.HIGHEST).reshape(NTR, LEV, NLAT, NLON)
    sea_mask = land_mask.astype(jnp.float32)
    mask_wide = extend(sea_mask)
    east_wide = extend(east_velocity)
    north_wide = extend(north_velocity)
    tracer_now = tracers
    for substep in range(NSUB):
        tracer_now = advect(extend(tracer_now), east_wide, north_wide, mask_wide)
    return tracer_now + sea_mask * source
```

```python
import functools

import jax
import jax.numpy as jnp
from jax import lax
from jax.experimental import pallas as pl
from jax.experimental.pallas import tpu as pltpu
from jax.sharding import PartitionSpec as P

NSUB = 4
DIFFUSION = 0.2
MESH = pl.DeviceIdType.MESH
F32 = jnp.float32


def offsets(step, n_lat, n_lon):
    ring = step // n_lat
    hop = (ring + 1) // 2
    d_lon = lax.rem(n_lon // 2 + jnp.where(ring % 2 == 1, -hop, hop) + n_lon, n_lon)
    d_lat = lax.rem(step + 1, n_lat)
    return d_lat, d_lon


def exchange_kernel(
    n_lat,
    n_lon,
    source_ref,
    target_ref,
    count_ref,
    atm_ref,
    weights_ref,
    tracers_ref,
    east_ref,
    north_ref,
    land_ref,
    flux_ref,
    rim_ref,
    rim_sea_ref,
    strip_ref,
    atm_blocks,
    weights,
    parts,
    arrived,
    marks,
    landed,
    sea,
    from_north,
    from_south,
    edge,
    from_east,
    from_west,
    weight_sem,
    part_send,
    part_recv,
    mark_send,
    mark_recv,
    lat_send,
    lat_recv,
    lon_send,
    lon_recv,
):
    lat, lon = lax.axis_index("lat"), lax.axis_index("lon")
    me = lat * n_lon + lon
    devices = n_lat * n_lon
    fields, block = atm_blocks.shape[1:]
    slots = marks.shape[1]
    levels, rows, cols = east_ref.shape
    tracer_count = tracers_ref.shape[0] // levels

    def partner(step):
        d_lat, d_lon = offsets(step, n_lat, n_lon)
        return lax.rem(lat + d_lat, n_lat), lax.rem(lon + d_lon, n_lon)

    def origin(step):
        d_lat, d_lon = offsets(step, n_lat, n_lon)
        return lax.rem(lat - d_lat + n_lat, n_lat) * n_lon + lax.rem(lon - d_lon + n_lon, n_lon)

    barrier = pltpu.get_barrier_semaphore()

    @pl.loop(0, devices - 1)
    def _(step):
        pl.semaphore_signal(barrier, inc=1, device_id=partner(step), device_id_type=MESH)

    def weight_copy(step):
        p_lat, p_lon = partner(step)
        tile = p_lat * n_lon + p_lon
        return pltpu.make_async_copy(
            weights_ref.at[pl.ds(tile * slots, slots)],
            weights.at[pl.ds(step * slots, slots)],
            weight_sem.at[step],
        )

    @pl.loop(0, devices)
    def _(step):
        weight_copy(step).start()

    for b in range(atm_blocks.shape[0]):
        atm_blocks[b] = atm_ref[:, b * block : (b + 1) * block].astype(F32)
    sea[...] = land_ref[...].astype(F32)

    @pl.loop(0, devices)
    def _(step):
        p_lat, p_lon = partner(step)
        tile = p_lat * n_lon + p_lon
        for k in range(slots):
            mark = jnp.where(k < count_ref[0, tile], target_ref[0, tile * slots + k], -1)
            marks[step, k] = jnp.full((1, block), mark, jnp.int32)

    pl.semaphore_wait(barrier, devices - 1)

    def lat_copies(north):
        first, to, into, way = (rows - 8, lat + 1, from_south, 0) if north else (0, lat - 1, from_north, 1)
        pieces = (
            (tracers_ref, into.at[pl.ds(0, tracer_count * levels)]),
            (east_ref, into.at[pl.ds(tracer_count * levels, levels)]),
            (north_ref, into.at[pl.ds((tracer_count + 1) * levels, levels)]),
        )
        copies = [
            pltpu.make_async_remote_copy(
                src_ref=ref.at[:, pl.ds(first, 8), :],
                dst_ref=dst,
                send_sem=lat_send.at[way, n],
                recv_sem=lat_recv.at[way, n],
                device_id=(to, lon),
                device_id_type=MESH,
            )
            for n, (ref, dst) in enumerate(pieces)
        ]
        copies.append(
            pltpu.make_async_remote_copy(
                src_ref=sea.at[pl.ds(first, 8), :],
                dst_ref=into.at[(tracer_count + 2) * levels],
                send_sem=lat_send.at[way, 3],
                recv_sem=lat_recv.at[way, 3],
                device_id=(to, lon),
                device_id_type=MESH,
            )
        )
        return copies

    @pl.when(lat < n_lat - 1)
    def _():
        for copy in lat_copies(True):
            copy.start()

    @pl.when(lat > 0)
    def _():
        for copy in lat_copies(False):
            copy.start()

    def mark_copy(step):
        return pltpu.make_async_remote_copy(
            src_ref=marks.at[step],
            dst_ref=landed.at[me],
            send_sem=mark_send.at[step],
            recv_sem=mark_recv.at[step],
            device_id=partner(step),
            device_id_type=MESH,
        )

    def part_copy(step):
        return pltpu.make_async_remote_copy(
            src_ref=parts.at[step],
            dst_ref=arrived.at[me],
            send_sem=part_send.at[step],
            recv_sem=part_recv.at[step],
            device_id=partner(step),
            device_id_type=MESH,
        )

    def remap(step, into, at):
        p_lat, p_lon = partner(step)
        tile = p_lat * n_lon + p_lon
        weight_copy(step).wait()
        for k in range(slots):
            chosen = atm_blocks[source_ref[0, tile * slots + k]].astype(jnp.bfloat16)
            into[at, k * fields : (k + 1) * fields, :] = jnp.dot(
                chosen, weights[step * slots + k], preferred_element_type=F32
            )

    @pl.loop(0, devices - 1)
    def _(step):
        mark_copy(step).start()

    def send(step):
        remap(step, parts, step)
        part_copy(step).start()

    half = devices // 2
    pl.loop(0, half)(send)

    planes = (tracer_count + 2) * levels + 1

    @pl.when(lat > 0)
    def _():
        for copy in lat_copies(True):
            copy.wait_recv()

    @pl.when(lat < n_lat - 1)
    def _():
        for copy in lat_copies(False):
            copy.wait_recv()

    @pl.when(lat == 0)
    def _():
        from_south[...] = jnp.zeros_like(from_south)

    @pl.when(lat == n_lat - 1)
    def _():
        from_north[...] = jnp.zeros_like(from_north)

    upper = lax.broadcasted_iota(jnp.int32, (8, cols), 0) < 4

    @pl.loop(0, planes - 1)
    def _(plane):
        rim_ref[plane] = jnp.where(upper, from_north[plane], from_south[plane])

    rim_sea_ref[...] = jnp.where(upper, from_north[planes - 1], from_south[planes - 1])

    width = cols // levels
    lane = lax.broadcasted_iota(jnp.int32, (rows + 8, cols), 1)
    groups = tracer_count + 3
    edge[...] = jnp.zeros_like(edge)

    @pl.loop(0, levels)
    def _(level):
        here = (lane >= level * width) & (lane < (level + 1) * width)
        shift = level * width + width // 2

        def put(group, inner, rim):
            moved = pltpu.roll(jnp.concatenate([inner, rim], axis=0), shift, 1)
            edge[group] = jnp.where(here, moved, edge[group])

        for t in range(tracer_count):
            put(t, tracers_ref[t * levels + level], rim_ref[t * levels + level])
        put(tracer_count, east_ref[level], rim_ref[tracer_count * levels + level])
        put(tracer_count + 1, north_ref[level], rim_ref[(tracer_count + 1) * levels + level])
        put(tracer_count + 2, sea[...], rim_sea_ref[...])

    def lon_copy(east):
        to, into, way = (lon + 1, from_west, 0) if east else (lon + n_lon - 1, from_east, 1)
        return pltpu.make_async_remote_copy(
            src_ref=edge,
            dst_ref=into,
            send_sem=lon_send.at[way],
            recv_sem=lon_recv.at[way],
            device_id=(lat, lax.rem(to, n_lon)),
            device_id_type=MESH,
        )

    lon_copy(True).start()
    lon_copy(False).start()

    pl.loop(half, devices - 1)(send)
    remap(devices - 1, arrived, me)
    landed[me] = marks[devices - 1]

    flux_ref[...] = jnp.zeros_like(flux_ref)

    def gather(source):
        for k in range(slots):
            mark = jnp.broadcast_to(landed[source, k], (8, block))
            for first in range(0, fields, 8):
                part = arrived[source, k * fields + first : k * fields + first + 8, :]
                for row in range(rows):
                    flux_ref[row, first : first + 8, :] += jnp.where(mark == row, part, 0.0)

    gather(me)

    lon_copy(True).wait_recv()
    lon_copy(False).wait_recv()
    west_side = lax.rem(lane, width) < width // 2

    @pl.loop(0, groups)
    def _(group):
        strip_ref[0, group] = jnp.where(west_side, edge[group], from_east[group])
        strip_ref[1, group] = jnp.where(west_side, from_west[group], edge[group])

    @pl.loop(0, devices - 1)
    def _(step):
        mark_copy(step).wait_recv()
        pltpu.make_async_remote_copy(
            src_ref=parts.at[step],
            dst_ref=arrived.at[origin(step)],
            send_sem=part_send.at[step],
            recv_sem=part_recv.at[step],
            device_id=partner(step),
            device_id_type=MESH,
        ).wait_recv()
        gather(origin(step))

    @pl.loop(0, devices - 1)
    def _(step):
        mark_copy(step).wait_send()
        part_copy(step).wait_send()

    @pl.when(lat < n_lat - 1)
    def _():
        for copy in lat_copies(True):
            copy.wait_send()

    @pl.when(lat > 0)
    def _():
        for copy in lat_copies(False):
            copy.wait_send()

    lon_copy(True).wait_send()
    lon_copy(False).wait_send()


def shifted(field):
    cols, rows = field.shape[1], field.shape[0]
    return (
        pltpu.roll(field, cols - 1, 1),
        pltpu.roll(field, 1, 1),
        pltpu.roll(field, rows - 1, 0),
        pltpu.roll(field, 1, 0),
    )


def faces(east, north, sea):
    sea_east = sea * pltpu.roll(sea, sea.shape[1] - 1, 1)
    sea_north = sea * pltpu.roll(sea, sea.shape[0] - 1, 0)
    return (
        sea_east * (0.5 * east + DIFFUSION),
        sea_east * (0.5 * east - DIFFUSION),
        sea_north * (0.5 * north + DIFFUSION),
        sea_north * (0.5 * north - DIFFUSION),
    )


def advect_kernel(
    tracers_ref,
    east_ref,
    north_ref,
    land_ref,
    rim_ref,
    rim_sea_ref,
    strip_ref,
    flux_ref,
    coupling_ref,
    out_ref,
    source,
    beyond,
    sides,
):
    levels, rows, cols = east_ref.shape
    tracer_count = tracers_ref.shape[0] // levels
    planes = tracer_count * levels
    width = cols // levels
    tall = (rows + 8, cols)
    lane = lax.broadcasted_iota(jnp.int32, tall, 1)
    place = lax.rem(lane, width)

    coupling = coupling_ref[...]
    lead = coupling.astype(jnp.bfloat16).astype(F32)
    factors = jnp.concatenate([lead, lead, coupling - lead], axis=1).astype(jnp.bfloat16)
    for row in range(rows):
        flux = flux_ref[row]
        head = flux.astype(jnp.bfloat16).astype(F32)
        stack = jnp.concatenate([head, flux - head, head], axis=0).astype(jnp.bfloat16)
        source[row * planes : (row + 1) * planes, :] = jnp.dot(
            factors, stack, preferred_element_type=F32
        )

    weights = []
    for side in range(2):
        sea = strip_ref[side, tracer_count + 2]
        a, b, c, d = faces(strip_ref[side, tracer_count], strip_ref[side, tracer_count + 1], sea)
        a_west, b_west = pltpu.roll(a, 1, 1), pltpu.roll(b, 1, 1)
        c_south, d_south = pltpu.roll(c, 1, 0), pltpu.roll(d, 1, 0)
        weights.append((1.0 - a + b_west - c + d_south, -b, a_west, -d, c_south))
        if side == 1:
            sides[0] = pltpu.roll(a, 1, 1)
            sides[1] = pltpu.roll(b, 1, 1)
        else:
            sides[2] = pltpu.roll(sea, cols - 1, 1)
    half = width // 2
    for t in range(tracer_count):
        now = [strip_ref[0, t], strip_ref[1, t]]
        for step in range(NSUB):
            east_of = pltpu.roll(now[0], cols - 1, 1)
            west_of = pltpu.roll(now[1], 1, 1)
            beyond[step, t] = jnp.where(place < half, east_of, west_of)
            if step < NSUB - 1:
                for side in range(2):
                    own, e, w, n, s = weights[side]
                    qe, qw, qn, qs = shifted(now[side])
                    now[side] = own * now[side] + e * qe + w * qw + n * qn + s * qs

    sea = jnp.concatenate([land_ref[...].astype(F32), rim_sea_ref[...]], axis=0)
    first, last = lane == 0, lane == cols - 1
    sea_here = sea[:rows]

    @pl.loop(0, levels)
    def _(level):
        shift = lax.rem(2 * cols - level * width - half, cols)
        east = jnp.concatenate([east_ref[level], rim_ref[planes + level]], axis=0)
        north = jnp.concatenate([north_ref[level], rim_ref[planes + levels + level]], axis=0)
        sea_beyond = pltpu.roll(sides[2], shift, 1)
        sea_east = sea * jnp.where(last, sea_beyond, pltpu.roll(sea, cols - 1, 1))
        _, _, c, d = faces(east, north, sea)
        a = sea_east * (0.5 * east + DIFFUSION)
        b = sea_east * (0.5 * east - DIFFUSION)
        a_west = jnp.where(first, pltpu.roll(sides[0], shift, 1), pltpu.roll(a, 1, 1))
        b_west = jnp.where(first, pltpu.roll(sides[1], shift, 1), pltpu.roll(b, 1, 1))
        c_south, d_south = pltpu.roll(c, 1, 0), pltpu.roll(d, 1, 0)
        own = 1.0 - a + b_west - c + d_south
        for t in range(tracer_count):
            plane = t * levels + level
            now = jnp.concatenate([tracers_ref[plane], rim_ref[plane]], axis=0)
            for step in range(NSUB):
                outer = pltpu.roll(beyond[step, t], shift, 1)
                qe, qw, qn, qs = shifted(now)
                qe, qw = jnp.where(last, outer, qe), jnp.where(first, outer, qw)
                now = own * now - b * qe + a_west * qw - d * qn + c_south * qs
            out_ref[plane] = now[:rows] + sea_here * source[pl.ds(plane, rows, planes), :]


def per_device(
    n_lat,
    n_lon,
    atm_fluxes,
    remap_weights,
    source_block,
    target_block,
    block_count,
    tracers,
    east_velocity,
    north_velocity,
    land_mask,
    coupling,
):
    fields, cells = atm_fluxes.shape
    block = remap_weights.shape[-1]
    devices = n_lat * n_lon
    slots = source_block.shape[1] // devices
    tracer_count, levels, rows, cols = tracers.shape
    planes = tracer_count * levels
    groups = tracer_count + 3
    tall = rows + 8
    flat = tracers.reshape(planes, rows, cols)
    vmem = pl.BlockSpec(memory_space=pltpu.VMEM)
    smem = pl.BlockSpec(memory_space=pltpu.SMEM)
    dma = pltpu.SemaphoreType.DMA
    shape = jax.ShapeDtypeStruct
    flux, rim, rim_sea, strip = pl.pallas_call(
        functools.partial(exchange_kernel, n_lat, n_lon),
        out_shape=(
            shape((rows, fields, block), F32),
            shape((planes + 2 * levels, 8, cols), F32),
            shape((8, cols), F32),
            shape((2, groups, tall, cols), F32),
        ),
        in_specs=[smem, smem, smem, vmem, pl.BlockSpec(memory_space=pl.ANY)] + [vmem] * 4,
        out_specs=(vmem,) * 4,
        scratch_shapes=[
            pltpu.VMEM((cells // block, fields, block), F32),
            pltpu.VMEM((devices * slots, block, block), jnp.bfloat16),
            pltpu.VMEM((devices, slots * fields, block), F32),
            pltpu.VMEM((devices, slots * fields, block), F32),
            pltpu.VMEM((devices, slots, 1, block), jnp.int32),
            pltpu.VMEM((devices, slots, 1, block), jnp.int32),
            pltpu.VMEM((rows, cols), F32),
            pltpu.VMEM((planes + 2 * levels + 1, 8, cols), F32),
            pltpu.VMEM((planes + 2 * levels + 1, 8, cols), F32),
            pltpu.VMEM((groups, tall, cols), F32),
            pltpu.VMEM((groups, tall, cols), F32),
            pltpu.VMEM((groups, tall, cols), F32),
            dma((devices,)),
            dma((devices,)),
            dma((devices,)),
            dma((devices,)),
            dma((devices,)),
            dma((2, 4)),
            dma((2, 4)),
            dma((2,)),
            dma((2,)),
        ],
        compiler_params=pltpu.CompilerParams(
            collective_id=0, has_side_effects=True, vmem_limit_bytes=40 * 1024 * 1024
        ),
    )(
        source_block,
        target_block,
        block_count,
        atm_fluxes,
        remap_weights.reshape(devices * slots, block, block),
        flat,
        east_velocity,
        north_velocity,
        land_mask,
    )
    out = pl.pallas_call(
        advect_kernel,
        out_shape=shape((planes, rows, cols), F32),
        in_specs=[vmem] * 9,
        out_specs=vmem,
        scratch_shapes=[
            pltpu.VMEM((rows * planes, cols), F32),
            pltpu.VMEM((NSUB, tracer_count, tall, cols), F32),
            pltpu.VMEM((3, tall, cols), F32),
        ],
        compiler_params=pltpu.CompilerParams(vmem_limit_bytes=40 * 1024 * 1024),
    )(flat, east_velocity, north_velocity, land_mask, rim, rim_sea, strip, flux, coupling)
    return out.reshape(tracers.shape)


def solution(mesh):
    placed = (
        P(None, ("lat", "lon")),
        P(("lat", "lon"), None, None, None),
        P(("lat", "lon"), None),
        P(("lat", "lon"), None),
        P(("lat", "lon"), None),
        P(None, None, "lat", "lon"),
        P(None, "lat", "lon"),
        P(None, "lat", "lon"),
        P("lat", "lon"),
        P(),
    )
    return jax.shard_map(
        functools.partial(per_device, mesh.shape["lat"], mesh.shape["lon"]),
        mesh=mesh,
        in_specs=placed,
        out_specs=P(None, None, "lat", "lon"),
        check_vma=False,
    )
```

```python
import functools

import jax
import jax.numpy as jnp
from jax import lax
from jax.experimental import pallas as pl
from jax.experimental.pallas import tpu as pltpu
from jax.sharding import PartitionSpec as P

NSUB = 4
DIFFUSION = 0.2
MESH = pl.DeviceIdType.MESH
F32 = jnp.float32


def offsets(step, n_lat, n_lon):
    ring = step // n_lat
    hop = (ring + 1) // 2
    d_lon = lax.rem(n_lon // 2 + jnp.where(ring % 2 == 1, -hop, hop) + n_lon, n_lon)
    d_lat = lax.rem(step + 1, n_lat)
    return d_lat, d_lon


def shifted(field):
    cols, rows = field.shape[1], field.shape[0]
    return (
        pltpu.roll(field, cols - 1, 1),
        pltpu.roll(field, 1, 1),
        pltpu.roll(field, rows - 1, 0),
        pltpu.roll(field, 1, 0),
    )


def faces(east, north, sea):
    sea_east = sea * pltpu.roll(sea, sea.shape[1] - 1, 1)
    sea_north = sea * pltpu.roll(sea, sea.shape[0] - 1, 0)
    return (
        sea_east * (0.5 * east + DIFFUSION),
        sea_east * (0.5 * east - DIFFUSION),
        sea_north * (0.5 * north + DIFFUSION),
        sea_north * (0.5 * north - DIFFUSION),
    )


def exchange_kernel(
    n_lat,
    n_lon,
    source_hbm,
    target_hbm,
    count_hbm,
    atm_hbm,
    weights_hbm,
    tracers_hbm,
    east_hbm,
    north_hbm,
    land_hbm,
    flux_ref,
    advected_hbm,
    source_ref,
    target_ref,
    count_ref,
    atm_ref,
    land_ref,
    advected_ref,
    atm_blocks,
    weights,
    parts,
    arrived,
    marks,
    landed,
    state,
    sea,
    to_north,
    to_south,
    from_north,
    from_south,
    edge,
    to_east,
    to_west,
    from_east,
    from_west,
    strip,
    beyond,
    sides,
    load_sem,
    weight_sem,
    part_send,
    part_recv,
    mark_send,
    mark_recv,
    lat_send,
    lat_recv,
    lon_send,
    lon_recv,
):
    lat, lon = lax.axis_index("lat"), lax.axis_index("lon")
    me = lat * n_lon + lon
    devices = n_lat * n_lon
    fields, block = atm_blocks.shape[1:]
    slots = marks.shape[1]
    planes, rows, cols = tracers_hbm.shape
    levels = east_hbm.shape[0]
    tracer_count = planes // levels
    total = planes + 2 * levels
    pairs = total // 2

    def partner(step):
        d_lat, d_lon = offsets(step, n_lat, n_lon)
        return lax.rem(lat + d_lat, n_lat), lax.rem(lon + d_lon, n_lon)

    def origin(step):
        d_lat, d_lon = offsets(step, n_lat, n_lon)
        return lax.rem(lat - d_lat + n_lat, n_lat) * n_lon + lax.rem(lon - d_lon + n_lon, n_lon)

    barrier = pltpu.get_barrier_semaphore()

    @pl.loop(0, devices - 1)
    def _(step):
        pl.semaphore_signal(barrier, inc=1, device_id=partner(step), device_id_type=MESH)

    inner = pl.ds(0, rows)
    loads = [
        pltpu.make_async_copy(a, b, load_sem.at[n])
        for n, (a, b) in enumerate(
            (
                (tracers_hbm, state.at[pl.ds(0, planes), inner, :]),
                (east_hbm, state.at[pl.ds(planes, levels), inner, :]),
                (north_hbm, state.at[pl.ds(planes + levels, levels), inner, :]),
                (land_hbm, land_ref),
                (source_hbm, source_ref),
                (target_hbm, target_ref),
                (count_hbm, count_ref),
                (atm_hbm, atm_ref),
            )
        )
    ]
    for load in loads:
        load.start()

    def weight_copy(step):
        p_lat, p_lon = partner(step)
        tile = p_lat * n_lon + p_lon
        return pltpu.make_async_copy(
            weights_hbm.at[pl.ds(tile * slots, slots)],
            weights.at[pl.ds(step * slots, slots)],
            weight_sem.at[step],
        )

    @pl.loop(0, devices)
    def _(step):
        weight_copy(step).start()

    for load in loads[:4]:
        load.wait()
    sea[0:rows, :] = land_ref[...].astype(F32)

    upper = lax.broadcasted_iota(jnp.int32, (8, cols), 0) < 4

    @pl.loop(0, pairs)
    def _(i):
        low, high = state[i, 0:8, :], state[i + pairs, 0:8, :]
        to_south[i] = jnp.where(upper, low, pltpu.roll(high, 4, 0))
        low, high = state[i, rows - 8 : rows, :], state[i + pairs, rows - 8 : rows, :]
        to_north[i] = jnp.where(upper, pltpu.roll(high, 4, 0), low)

    to_south[pairs] = sea[0:8, :]
    to_north[pairs] = sea[rows - 8 : rows, :]
    pl.semaphore_wait(barrier, devices - 1)

    def lat_copy(north):
        ref, into, to, way = (
            (to_north, from_south, lat + 1, 0) if north else (to_south, from_north, lat - 1, 1)
        )
        return pltpu.make_async_remote_copy(
            src_ref=ref,
            dst_ref=into,
            send_sem=lat_send.at[way],
            recv_sem=lat_recv.at[way],
            device_id=(to, lon),
            device_id_type=MESH,
        )

    @pl.when(lat < n_lat - 1)
    def _():
        lat_copy(True).start()

    @pl.when(lat > 0)
    def _():
        lat_copy(False).start()

    for load in loads[4:]:
        load.wait()
    for b in range(atm_blocks.shape[0]):
        atm_blocks[b] = atm_ref[:, b * block : (b + 1) * block].astype(F32)

    def mark_copy(step):
        return pltpu.make_async_remote_copy(
            src_ref=marks.at[step],
            dst_ref=landed.at[me],
            send_sem=mark_send.at[step],
            recv_sem=mark_recv.at[step],
            device_id=partner(step),
            device_id_type=MESH,
        )

    def part_copy(step):
        return pltpu.make_async_remote_copy(
            src_ref=parts.at[step],
            dst_ref=arrived.at[me],
            send_sem=part_send.at[step],
            recv_sem=part_recv.at[step],
            device_id=partner(step),
            device_id_type=MESH,
        )

    def remap(step, into, at):
        p_lat, p_lon = partner(step)
        tile = p_lat * n_lon + p_lon
        weight_copy(step).wait()
        for k in range(slots):
            mark = jnp.where(k < count_ref[0, tile], target_ref[0, tile * slots + k], -1)
            marks[step, k] = jnp.full((1, block), mark, jnp.int32)
            chosen = atm_blocks[source_ref[0, tile * slots + k]].astype(jnp.bfloat16)
            into[at, k * fields : (k + 1) * fields, :] = jnp.dot(
                chosen, weights[step * slots + k], preferred_element_type=F32
            )

    def send(step):
        remap(step, parts, step)
        mark_copy(step).start()
        part_copy(step).start()

    early = 3 * devices // 8
    pl.loop(0, early)(send)

    @pl.when(lat > 0)
    def _():
        lat_copy(True).wait_recv()

    @pl.when(lat < n_lat - 1)
    def _():
        lat_copy(False).wait_recv()

    @pl.when(lat == 0)
    def _():
        from_south[...] = jnp.zeros_like(from_south)

    @pl.when(lat == n_lat - 1)
    def _():
        from_north[...] = jnp.zeros_like(from_north)

    @pl.loop(0, pairs)
    def _(i):
        north, south = from_north[i], from_south[i]
        state[i, rows:, :] = jnp.where(upper, north, south)
        state[i + pairs, rows:, :] = pltpu.roll(jnp.where(upper, south, north), 4, 0)

    sea[rows:, :] = jnp.where(upper, from_north[pairs], from_south[pairs])

    width = cols // levels
    near = width // 2
    groups = tracer_count + 3
    joint = groups // 2
    lane = lax.broadcasted_iota(jnp.int32, (rows + 8, cols), 1)
    place = lax.rem(lane, width)
    west_side = place < near
    edge[...] = jnp.zeros_like(edge)

    @pl.loop(0, levels)
    def _(level):
        here = (lane >= level * width) & (lane < (level + 1) * width)
        shift = level * width + near
        for group in range(groups):
            field = state[group * levels + level] if group < groups - 1 else sea[...]
            edge[group] = jnp.where(here, pltpu.roll(field, shift, 1), edge[group])

    for group in range(joint):
        low, high = edge[group], edge[group + joint]
        to_east[group] = jnp.where(west_side, low, pltpu.roll(high, near, 1))
        to_west[group] = jnp.where(west_side, pltpu.roll(high, cols - near, 1), low)
    to_east[joint] = edge[groups - 1]
    to_west[joint] = edge[groups - 1]

    def lon_copy(east):
        ref, into, to, way = (
            (to_east, from_west, lon + 1, 0) if east else (to_west, from_east, lon + n_lon - 1, 1)
        )
        return pltpu.make_async_remote_copy(
            src_ref=ref,
            dst_ref=into,
            send_sem=lon_send.at[way],
            recv_sem=lon_recv.at[way],
            device_id=(lat, lax.rem(to, n_lon)),
            device_id_type=MESH,
        )

    lon_copy(True).start()
    lon_copy(False).start()

    pl.loop(early, devices - 1)(send)
    remap(devices - 1, arrived, me)
    landed[me] = marks[devices - 1]

    flux_ref[...] = jnp.zeros_like(flux_ref)

    def gather(source):
        seen = [jnp.broadcast_to(landed[source, k], (8, block)) for k in range(slots)]
        for first in range(0, fields, 8):
            part = [
                arrived[source, k * fields + first : k * fields + first + 8, :]
                for k in range(slots)
            ]
            for row in range(rows):
                added = flux_ref[row, first : first + 8, :]
                for k in range(slots):
                    added = added + jnp.where(seen[k] == row, part[k], 0.0)
                flux_ref[row, first : first + 8, :] = added

    gather(me)

    lon_copy(True).wait_recv()
    lon_copy(False).wait_recv()
    for group in range(joint):
        low, high = edge[group], edge[group + joint]
        east, west = from_east[group], from_west[group]
        strip[0, group] = jnp.where(west_side, low, east)
        strip[0, group + joint] = jnp.where(west_side, high, pltpu.roll(east, near, 1))
        strip[1, group] = jnp.where(west_side, west, low)
        strip[1, group + joint] = jnp.where(west_side, pltpu.roll(west, cols - near, 1), high)
    strip[0, groups - 1] = jnp.where(west_side, edge[groups - 1], from_east[joint])
    strip[1, groups - 1] = jnp.where(west_side, from_west[joint], edge[groups - 1])

    stencils = []
    for side in range(2):
        sea_strip = strip[side, groups - 1]
        a, b, c, d = faces(strip[side, tracer_count], strip[side, tracer_count + 1], sea_strip)
        a_west, b_west = pltpu.roll(a, 1, 1), pltpu.roll(b, 1, 1)
        c_south, d_south = pltpu.roll(c, 1, 0), pltpu.roll(d, 1, 0)
        stencils.append((1.0 - a + b_west - c + d_south, -b, a_west, -d, c_south))
        if side == 1:
            sides[0] = a_west
            sides[1] = b_west
        else:
            sides[2] = pltpu.roll(sea_strip, cols - 1, 1)

    @pl.loop(0, tracer_count)
    def _(t):
        now = [strip[0, t], strip[1, t]]
        for step in range(NSUB):
            east_of = pltpu.roll(now[0], cols - 1, 1)
            west_of = pltpu.roll(now[1], 1, 1)
            beyond[step, t] = jnp.where(west_side, east_of, west_of)
            if step < NSUB - 1:
                for side in range(2):
                    own, e, w, n, s = stencils[side]
                    qe, qw, qn, qs = shifted(now[side])
                    now[side] = own * now[side] + e * qe + w * qw + n * qn + s * qs

    first_lane, last_lane = lane == 0, lane == cols - 1
    sea_all = sea[...]

    @pl.loop(0, levels)
    def _(level):
        shift = lax.rem(2 * cols - level * width - near, cols)
        east, north = state[planes + level], state[planes + levels + level]
        sea_beyond = pltpu.roll(sides[2], shift, 1)
        sea_east = sea_all * jnp.where(last_lane, sea_beyond, pltpu.roll(sea_all, cols - 1, 1))
        _, _, c, d = faces(east, north, sea_all)
        a = sea_east * (0.5 * east + DIFFUSION)
        b = sea_east * (0.5 * east - DIFFUSION)
        a_west = jnp.where(first_lane, pltpu.roll(sides[0], shift, 1), pltpu.roll(a, 1, 1))
        b_west = jnp.where(first_lane, pltpu.roll(sides[1], shift, 1), pltpu.roll(b, 1, 1))
        c_south, d_south = pltpu.roll(c, 1, 0), pltpu.roll(d, 1, 0)
        own = 1.0 - a + b_west - c + d_south
        for t in range(tracer_count):
            now = state[t * levels + level]
            for step in range(NSUB):
                outer = pltpu.roll(beyond[step, t], shift, 1)
                qe, qw, qn, qs = shifted(now)
                qe, qw = jnp.where(last_lane, outer, qe), jnp.where(first_lane, outer, qw)
                now = own * now - b * qe + a_west * qw - d * qn + c_south * qs
            advected_ref[t * levels + level] = now[:rows]

    saved = pltpu.make_async_copy(advected_ref, advected_hbm, load_sem.at[0])
    saved.start()

    @pl.loop(0, devices - 1)
    def _(step):
        mark_copy(step).wait_recv()
        pltpu.make_async_remote_copy(
            src_ref=parts.at[step],
            dst_ref=arrived.at[origin(step)],
            send_sem=part_send.at[step],
            recv_sem=part_recv.at[step],
            device_id=partner(step),
            device_id_type=MESH,
        ).wait_recv()
        gather(origin(step))

    @pl.loop(0, devices - 1)
    def _(step):
        mark_copy(step).wait_send()
        part_copy(step).wait_send()

    @pl.when(lat < n_lat - 1)
    def _():
        lat_copy(True).wait_send()

    @pl.when(lat > 0)
    def _():
        lat_copy(False).wait_send()

    lon_copy(True).wait_send()
    lon_copy(False).wait_send()
    saved.wait()


def couple_kernel(
    flux_hbm,
    land_hbm,
    coupling_hbm,
    advected_hbm,
    out_ref,
    flux_ref,
    land_ref,
    coupling_ref,
    advected_ref,
    source,
    result,
    load_sem,
    sem,
):
    rows, cols = land_ref.shape
    planes = advected_ref.shape[0]
    pieces = sem.shape[0]
    share = planes // pieces
    loads = [
        pltpu.make_async_copy(a, b, load_sem.at[n])
        for n, (a, b) in enumerate(
            (
                (flux_hbm, flux_ref),
                (land_hbm, land_ref),
                (coupling_hbm, coupling_ref),
                (advected_hbm, advected_ref),
            )
        )
    ]
    for load in loads:
        load.start()
    for load in loads[:3]:
        load.wait()
    coupling = coupling_ref[...]
    lead = coupling.astype(jnp.bfloat16).astype(F32)
    factors = jnp.concatenate([lead, lead, coupling - lead], axis=0).astype(jnp.bfloat16)
    for row in range(rows):
        flux = flux_ref[row]
        head = flux.astype(jnp.bfloat16).astype(F32)
        stack = jnp.concatenate([head, flux - head, head], axis=0).astype(jnp.bfloat16)
        source[row * planes : (row + 1) * planes, :] = lax.dot_general(
            factors, stack, (((0,), (0,)), ((), ())), preferred_element_type=F32
        )
    sea = land_ref[...].astype(F32)
    loads[3].wait()
    copies = []
    for piece in range(pieces):
        for plane in range(piece * share, (piece + 1) * share):
            added = source[pl.ds(plane, rows, planes), :]
            result[plane] = advected_ref[plane] + sea * added
        here = pl.ds(piece * share, share)
        copies.append(pltpu.make_async_copy(result.at[here], out_ref.at[here], sem.at[piece]))
        copies[-1].start()
    for copy in copies:
        copy.wait()


def per_device(
    n_lat,
    n_lon,
    atm_fluxes,
    remap_weights,
    source_block,
    target_block,
    block_count,
    tracers,
    east_velocity,
    north_velocity,
    land_mask,
    coupling,
):
    fields, cells = atm_fluxes.shape
    block = remap_weights.shape[-1]
    devices = n_lat * n_lon
    slots = source_block.shape[1] // devices
    tracer_count, levels, rows, cols = tracers.shape
    planes = tracer_count * levels
    groups = tracer_count + 3
    tall = rows + 8
    pairs = planes // 2 + levels
    vmem = pl.BlockSpec(memory_space=pltpu.VMEM)
    anywhere = pl.BlockSpec(memory_space=pl.ANY)
    dma = pltpu.SemaphoreType.DMA
    shape = jax.ShapeDtypeStruct
    flux, advected = pl.pallas_call(
        functools.partial(exchange_kernel, n_lat, n_lon),
        out_shape=(
            shape((rows, fields, block), F32),
            shape((planes, rows, cols), F32),
        ),
        in_specs=[anywhere] * 9,
        out_specs=(vmem, anywhere),
        scratch_shapes=[
            pltpu.SMEM(source_block.shape, jnp.int32),
            pltpu.SMEM(target_block.shape, jnp.int32),
            pltpu.SMEM(block_count.shape, jnp.int32),
            pltpu.VMEM((fields, cells), jnp.bfloat16),
            pltpu.VMEM((rows, cols), jnp.int32),
            pltpu.VMEM((planes, rows, cols), F32),
            pltpu.VMEM((cells // block, fields, block), F32),
            pltpu.VMEM((devices * slots, block, block), jnp.bfloat16),
            pltpu.VMEM((devices, slots * fields, block), F32),
            pltpu.VMEM((devices, slots * fields, block), F32),
            pltpu.VMEM((devices, slots, 1, block), jnp.int32),
            pltpu.VMEM((devices, slots, 1, block), jnp.int32),
            pltpu.VMEM((planes + 2 * levels, tall, cols), F32),
            pltpu.VMEM((tall, cols), F32),
        ]
        + [pltpu.VMEM((pairs + 1, 8, cols), F32)] * 4
        + [pltpu.VMEM((groups, tall, cols), F32)]
        + [pltpu.VMEM((groups // 2 + 1, tall, cols), F32)] * 4
        + [
            pltpu.VMEM((2, groups, tall, cols), F32),
            pltpu.VMEM((NSUB, tracer_count, tall, cols), F32),
            pltpu.VMEM((3, tall, cols), F32),
            dma((8,)),
            dma((devices,)),
            dma((devices,)),
            dma((devices,)),
            dma((devices,)),
            dma((devices,)),
            dma((2,)),
            dma((2,)),
            dma((2,)),
            dma((2,)),
        ],
        compiler_params=pltpu.CompilerParams(
            collective_id=0, has_side_effects=True, vmem_limit_bytes=60 * 1024 * 1024
        ),
    )(
        source_block,
        target_block,
        block_count,
        atm_fluxes,
        remap_weights.reshape(devices * slots, block, block),
        tracers.reshape(planes, rows, cols),
        east_velocity,
        north_velocity,
        land_mask,
    )
    out = pl.pallas_call(
        couple_kernel,
        out_shape=shape((planes, rows, cols), F32),
        in_specs=[anywhere] * 4,
        out_specs=anywhere,
        scratch_shapes=[
            pltpu.VMEM((rows, fields, block), F32),
            pltpu.VMEM((rows, cols), jnp.int32),
            pltpu.VMEM((fields, planes), F32),
            pltpu.VMEM((planes, rows, cols), F32),
            pltpu.VMEM((rows * planes, cols), F32),
            pltpu.VMEM((planes, rows, cols), F32),
            dma((4,)),
            dma((tracer_count,)),
        ],
        compiler_params=pltpu.CompilerParams(vmem_limit_bytes=60 * 1024 * 1024),
    )(flux, land_mask, coupling.T, advected)
    return out.reshape(tracers.shape)


def solution(mesh):
    placed = (
        P(None, ("lat", "lon")),
        P(("lat", "lon"), None, None, None),
        P(("lat", "lon"), None),
        P(("lat", "lon"), None),
        P(("lat", "lon"), None),
        P(None, None, "lat", "lon"),
        P(None, "lat", "lon"),
        P(None, "lat", "lon"),
        P("lat", "lon"),
        P(),
    )
    return jax.shard_map(
        functools.partial(per_device, mesh.shape["lat"], mesh.shape["lon"]),
        mesh=mesh,
        in_specs=placed,
        out_specs=P(None, None, "lat", "lon"),
        check_vma=False,
    )
```

```python
import functools

import jax
import jax.numpy as jnp
from jax import lax
from jax.experimental import pallas as pl
from jax.experimental.pallas import tpu as pltpu
from jax.sharding import PartitionSpec as P

NSUB = 4
DIFFUSION = 0.2
MESH = pl.DeviceIdType.MESH
F32 = jnp.float32


def offsets(step, n_lat, n_lon):
    ring = step // n_lat
    hop = (ring + 1) // 2
    d_lon = lax.rem(n_lon // 2 + jnp.where(ring % 2 == 1, -hop, hop) + n_lon, n_lon)
    d_lat = lax.rem(step + 1, n_lat)
    return d_lat, d_lon


def shifted(field):
    cols, rows = field.shape[1], field.shape[0]
    return (
        pltpu.roll(field, cols - 1, 1),
        pltpu.roll(field, 1, 1),
        pltpu.roll(field, rows - 1, 0),
        pltpu.roll(field, 1, 0),
    )


def faces(east, north, sea):
    sea_east = sea * pltpu.roll(sea, sea.shape[1] - 1, 1)
    sea_north = sea * pltpu.roll(sea, sea.shape[0] - 1, 0)
    return (
        sea_east * (0.5 * east + DIFFUSION),
        sea_east * (0.5 * east - DIFFUSION),
        sea_north * (0.5 * north + DIFFUSION),
        sea_north * (0.5 * north - DIFFUSION),
    )


def exchange_kernel(
    n_lat,
    n_lon,
    source_hbm,
    target_hbm,
    count_hbm,
    atm_hbm,
    weights_hbm,
    tracers_hbm,
    east_hbm,
    north_hbm,
    land_hbm,
    flux_ref,
    advected_hbm,
    source_ref,
    target_ref,
    count_ref,
    atm_ref,
    land_ref,
    advected_ref,
    atm_blocks,
    weights,
    parts,
    arrived,
    marks,
    landed,
    state,
    sea,
    to_north,
    to_south,
    from_north,
    from_south,
    edge,
    to_east,
    to_west,
    from_east,
    from_west,
    strip,
    beyond,
    sides,
    load_sem,
    weight_sem,
    part_send,
    part_recv,
    mark_send,
    mark_recv,
    lat_send,
    lat_recv,
    lon_send,
    lon_recv,
):
    lat, lon = lax.axis_index("lat"), lax.axis_index("lon")
    me = lat * n_lon + lon
    devices = n_lat * n_lon
    fields, block = atm_blocks.shape[1:]
    slots = marks.shape[1]
    planes, rows, cols = tracers_hbm.shape
    levels = east_hbm.shape[0]
    tracer_count = planes // levels
    total = planes + 2 * levels
    pairs = total // 2

    def partner(step):
        d_lat, d_lon = offsets(step, n_lat, n_lon)
        return lax.rem(lat + d_lat, n_lat), lax.rem(lon + d_lon, n_lon)

    def origin(step):
        d_lat, d_lon = offsets(step, n_lat, n_lon)
        return lax.rem(lat - d_lat + n_lat, n_lat) * n_lon + lax.rem(lon - d_lon + n_lon, n_lon)

    barrier = pltpu.get_barrier_semaphore()

    @pl.loop(0, devices - 1)
    def _(step):
        pl.semaphore_signal(barrier, inc=1, device_id=partner(step), device_id_type=MESH)

    inner = pl.ds(0, rows)
    loads = [
        pltpu.make_async_copy(a, b, load_sem.at[n])
        for n, (a, b) in enumerate(
            (
                (tracers_hbm, state.at[pl.ds(0, planes), inner, :]),
                (east_hbm, state.at[pl.ds(planes, levels), inner, :]),
                (north_hbm, state.at[pl.ds(planes + levels, levels), inner, :]),
                (land_hbm, land_ref),
                (source_hbm, source_ref),
                (target_hbm, target_ref),
                (count_hbm, count_ref),
                (atm_hbm, atm_ref),
            )
        )
    ]
    for load in loads:
        load.start()

    def weight_copy(step):
        p_lat, p_lon = partner(step)
        tile = p_lat * n_lon + p_lon
        return pltpu.make_async_copy(
            weights_hbm.at[pl.ds(tile * slots, slots)],
            weights.at[pl.ds(step * slots, slots)],
            weight_sem.at[step],
        )

    @pl.loop(0, devices)
    def _(step):
        weight_copy(step).start()

    for load in loads[:4]:
        load.wait()
    sea[0:rows, :] = land_ref[...].astype(F32)

    upper = lax.broadcasted_iota(jnp.int32, (8, cols), 0) < 4

    @pl.loop(0, pairs)
    def _(i):
        low, high = state[i, 0:8, :], state[i + pairs, 0:8, :]
        to_south[i] = jnp.where(upper, low, pltpu.roll(high, 4, 0))
        low, high = state[i, rows - 8 : rows, :], state[i + pairs, rows - 8 : rows, :]
        to_north[i] = jnp.where(upper, pltpu.roll(high, 4, 0), low)

    to_south[pairs] = sea[0:8, :]
    to_north[pairs] = sea[rows - 8 : rows, :]
    pl.semaphore_wait(barrier, devices - 1)

    def lat_copy(north):
        ref, into, to, way = (
            (to_north, from_south, lat + 1, 0) if north else (to_south, from_north, lat - 1, 1)
        )
        return pltpu.make_async_remote_copy(
            src_ref=ref,
            dst_ref=into,
            send_sem=lat_send.at[way],
            recv_sem=lat_recv.at[way],
            device_id=(to, lon),
            device_id_type=MESH,
        )

    @pl.when(lat < n_lat - 1)
    def _():
        lat_copy(True).start()

    @pl.when(lat > 0)
    def _():
        lat_copy(False).start()

    for load in loads[4:]:
        load.wait()
    for b in range(atm_blocks.shape[0]):
        atm_blocks[b] = atm_ref[:, b * block : (b + 1) * block].astype(F32)

    def mark_copy(step):
        return pltpu.make_async_remote_copy(
            src_ref=marks.at[step],
            dst_ref=landed.at[me],
            send_sem=mark_send.at[step],
            recv_sem=mark_recv.at[step],
            device_id=partner(step),
            device_id_type=MESH,
        )

    def part_copy(step):
        return pltpu.make_async_remote_copy(
            src_ref=parts.at[step],
            dst_ref=arrived.at[me],
            send_sem=part_send.at[step],
            recv_sem=part_recv.at[step],
            device_id=partner(step),
            device_id_type=MESH,
        )

    def remap(step, into, at):
        p_lat, p_lon = partner(step)
        tile = p_lat * n_lon + p_lon
        weight_copy(step).wait()
        for k in range(slots):
            mark = jnp.where(k < count_ref[0, tile], target_ref[0, tile * slots + k], -1)
            marks[step, k] = jnp.full((1, block), mark, jnp.int32)
            chosen = atm_blocks[source_ref[0, tile * slots + k]].astype(jnp.bfloat16)
            into[at, k * fields : (k + 1) * fields, :] = jnp.dot(
                chosen, weights[step * slots + k], preferred_element_type=F32
            )

    def send(step):
        remap(step, parts, step)
        mark_copy(step).start()
        part_copy(step).start()

    early = devices // 8
    pl.loop(0, early)(send)

    @pl.when(lat > 0)
    def _():
        lat_copy(True).wait_recv()

    @pl.when(lat < n_lat - 1)
    def _():
        lat_copy(False).wait_recv()

    @pl.when(lat == 0)
    def _():
        from_south[...] = jnp.zeros_like(from_south)

    @pl.when(lat == n_lat - 1)
    def _():
        from_north[...] = jnp.zeros_like(from_north)

    @pl.loop(0, pairs)
    def _(i):
        north, south = from_north[i], from_south[i]
        state[i, rows:, :] = jnp.where(upper, north, south)
        state[i + pairs, rows:, :] = pltpu.roll(jnp.where(upper, south, north), 4, 0)

    sea[rows:, :] = jnp.where(upper, from_north[pairs], from_south[pairs])

    width = cols // levels
    near = width // 2
    groups = tracer_count + 3
    joint = groups // 2
    lane = lax.broadcasted_iota(jnp.int32, (rows + 8, cols), 1)
    place = lax.rem(lane, width)
    west_side = place < near
    edge[...] = jnp.zeros_like(edge)

    @pl.loop(0, levels)
    def _(level):
        here = (lane >= level * width) & (lane < (level + 1) * width)
        shift = level * width + near
        for group in range(groups):
            field = state[group * levels + level] if group < groups - 1 else sea[...]
            edge[group] = jnp.where(here, pltpu.roll(field, shift, 1), edge[group])

    for group in range(joint):
        low, high = edge[group], edge[group + joint]
        to_east[group] = jnp.where(west_side, low, pltpu.roll(high, near, 1))
        to_west[group] = jnp.where(west_side, pltpu.roll(high, cols - near, 1), low)
    to_east[joint] = edge[groups - 1]
    to_west[joint] = edge[groups - 1]

    def lon_copy(east):
        ref, into, to, way = (
            (to_east, from_west, lon + 1, 0) if east else (to_west, from_east, lon + n_lon - 1, 1)
        )
        return pltpu.make_async_remote_copy(
            src_ref=ref,
            dst_ref=into,
            send_sem=lon_send.at[way],
            recv_sem=lon_recv.at[way],
            device_id=(lat, lax.rem(to, n_lon)),
            device_id_type=MESH,
        )

    lon_copy(True).start()
    lon_copy(False).start()

    pl.loop(early, devices - 1)(send)
    remap(devices - 1, arrived, me)
    landed[me] = marks[devices - 1]

    flux_ref[...] = jnp.zeros_like(flux_ref)

    def gather(source):
        seen = [jnp.broadcast_to(landed[source, k], (8, block)) for k in range(slots)]
        for first in range(0, fields, 8):
            part = [
                arrived[source, k * fields + first : k * fields + first + 8, :]
                for k in range(slots)
            ]
            for row in range(rows):
                added = flux_ref[row, first : first + 8, :]
                for k in range(slots):
                    added = added + jnp.where(seen[k] == row, part[k], 0.0)
                flux_ref[row, first : first + 8, :] = added

    gather(me)

    lon_copy(True).wait_recv()
    lon_copy(False).wait_recv()
    for group in range(joint):
        low, high = edge[group], edge[group + joint]
        east, west = from_east[group], from_west[group]
        strip[0, group] = jnp.where(west_side, low, east)
        strip[0, group + joint] = jnp.where(west_side, high, pltpu.roll(east, near, 1))
        strip[1, group] = jnp.where(west_side, west, low)
        strip[1, group + joint] = jnp.where(west_side, pltpu.roll(west, cols - near, 1), high)
    strip[0, groups - 1] = jnp.where(west_side, edge[groups - 1], from_east[joint])
    strip[1, groups - 1] = jnp.where(west_side, from_west[joint], edge[groups - 1])

    stencils = []
    for side in range(2):
        sea_strip = strip[side, groups - 1]
        a, b, c, d = faces(strip[side, tracer_count], strip[side, tracer_count + 1], sea_strip)
        a_west, b_west = pltpu.roll(a, 1, 1), pltpu.roll(b, 1, 1)
        c_south, d_south = pltpu.roll(c, 1, 0), pltpu.roll(d, 1, 0)
        stencils.append((1.0 - a + b_west - c + d_south, -b, a_west, -d, c_south))
        if side == 1:
            sides[0] = a_west
            sides[1] = b_west
        else:
            sides[2] = pltpu.roll(sea_strip, cols - 1, 1)

    @pl.loop(0, tracer_count)
    def _(t):
        now = [strip[0, t], strip[1, t]]
        for step in range(NSUB):
            east_of = pltpu.roll(now[0], cols - 1, 1)
            west_of = pltpu.roll(now[1], 1, 1)
            beyond[step, t] = jnp.where(west_side, east_of, west_of)
            if step < NSUB - 1:
                for side in range(2):
                    own, e, w, n, s = stencils[side]
                    qe, qw, qn, qs = shifted(now[side])
                    now[side] = own * now[side] + e * qe + w * qw + n * qn + s * qs

    first_lane, last_lane = lane == 0, lane == cols - 1
    sea_all = sea[...]

    @pl.loop(0, levels)
    def _(level):
        shift = lax.rem(2 * cols - level * width - near, cols)
        east, north = state[planes + level], state[planes + levels + level]
        sea_beyond = pltpu.roll(sides[2], shift, 1)
        sea_east = sea_all * jnp.where(last_lane, sea_beyond, pltpu.roll(sea_all, cols - 1, 1))
        _, _, c, d = faces(east, north, sea_all)
        a = sea_east * (0.5 * east + DIFFUSION)
        b = sea_east * (0.5 * east - DIFFUSION)
        a_west = jnp.where(first_lane, pltpu.roll(sides[0], shift, 1), pltpu.roll(a, 1, 1))
        b_west = jnp.where(first_lane, pltpu.roll(sides[1], shift, 1), pltpu.roll(b, 1, 1))
        c_south, d_south = pltpu.roll(c, 1, 0), pltpu.roll(d, 1, 0)
        own = 1.0 - a + b_west - c + d_south
        for t in range(tracer_count):
            now = state[t * levels + level]
            for step in range(NSUB):
                outer = pltpu.roll(beyond[step, t], shift, 1)
                qe, qw, qn, qs = shifted(now)
                qe, qw = jnp.where(last_lane, outer, qe), jnp.where(first_lane, outer, qw)
                now = own * now - b * qe + a_west * qw - d * qn + c_south * qs
            advected_ref[t * levels + level] = now[:rows]

    saved = pltpu.make_async_copy(advected_ref, advected_hbm, load_sem.at[0])
    saved.start()

    @pl.loop(0, devices - 1)
    def _(step):
        mark_copy(step).wait_recv()
        pltpu.make_async_remote_copy(
            src_ref=parts.at[step],
            dst_ref=arrived.at[origin(step)],
            send_sem=part_send.at[step],
            recv_sem=part_recv.at[step],
            device_id=partner(step),
            device_id_type=MESH,
        ).wait_recv()
        gather(origin(step))

    @pl.loop(0, devices - 1)
    def _(step):
        mark_copy(step).wait_send()
        part_copy(step).wait_send()

    @pl.when(lat < n_lat - 1)
    def _():
        lat_copy(True).wait_send()

    @pl.when(lat > 0)
    def _():
        lat_copy(False).wait_send()

    lon_copy(True).wait_send()
    lon_copy(False).wait_send()
    saved.wait()


def couple_kernel(
    flux_hbm,
    land_hbm,
    coupling_hbm,
    advected_hbm,
    out_ref,
    flux_ref,
    land_ref,
    coupling_ref,
    advected_ref,
    source,
    result,
    load_sem,
    sem,
):
    rows, cols = land_ref.shape
    planes = advected_ref.shape[0]
    pieces = sem.shape[0]
    share = planes // pieces
    loads = [
        pltpu.make_async_copy(a, b, load_sem.at[n])
        for n, (a, b) in enumerate(
            (
                (flux_hbm, flux_ref),
                (land_hbm, land_ref),
                (coupling_hbm, coupling_ref),
                (advected_hbm, advected_ref),
            )
        )
    ]
    for load in loads:
        load.start()
    for load in loads[:3]:
        load.wait()
    coupling = coupling_ref[...]
    lead = coupling.astype(jnp.bfloat16).astype(F32)
    factors = jnp.concatenate([lead, lead, coupling - lead], axis=0).astype(jnp.bfloat16)
    for row in range(rows):
        flux = flux_ref[row]
        head = flux.astype(jnp.bfloat16).astype(F32)
        stack = jnp.concatenate([head, flux - head, head], axis=0).astype(jnp.bfloat16)
        source[row * planes : (row + 1) * planes, :] = lax.dot_general(
            factors, stack, (((0,), (0,)), ((), ())), preferred_element_type=F32
        )
    sea = land_ref[...].astype(F32)
    loads[3].wait()
    copies = []
    for piece in range(pieces):
        for plane in range(piece * share, (piece + 1) * share):
            added = source[pl.ds(plane, rows, planes), :]
            result[plane] = advected_ref[plane] + sea * added
        here = pl.ds(piece * share, share)
        copies.append(pltpu.make_async_copy(result.at[here], out_ref.at[here], sem.at[piece]))
        copies[-1].start()
    for copy in copies:
        copy.wait()


def per_device(
    n_lat,
    n_lon,
    atm_fluxes,
    remap_weights,
    source_block,
    target_block,
    block_count,
    tracers,
    east_velocity,
    north_velocity,
    land_mask,
    coupling,
):
    fields, cells = atm_fluxes.shape
    block = remap_weights.shape[-1]
    devices = n_lat * n_lon
    slots = source_block.shape[1] // devices
    tracer_count, levels, rows, cols = tracers.shape
    planes = tracer_count * levels
    groups = tracer_count + 3
    tall = rows + 8
    pairs = planes // 2 + levels
    vmem = pl.BlockSpec(memory_space=pltpu.VMEM)
    anywhere = pl.BlockSpec(memory_space=pl.ANY)
    dma = pltpu.SemaphoreType.DMA
    shape = jax.ShapeDtypeStruct
    flux, advected = pl.pallas_call(
        functools.partial(exchange_kernel, n_lat, n_lon),
        out_shape=(
            shape((rows, fields, block), F32),
            shape((planes, rows, cols), F32),
        ),
        in_specs=[anywhere] * 9,
        out_specs=(vmem, anywhere),
        scratch_shapes=[
            pltpu.SMEM(source_block.shape, jnp.int32),
            pltpu.SMEM(target_block.shape, jnp.int32),
            pltpu.SMEM(block_count.shape, jnp.int32),
            pltpu.VMEM((fields, cells), jnp.bfloat16),
            pltpu.VMEM((rows, cols), jnp.int32),
            pltpu.VMEM((planes, rows, cols), F32),
            pltpu.VMEM((cells // block, fields, block), F32),
            pltpu.VMEM((devices * slots, block, block), jnp.bfloat16),
            pltpu.VMEM((devices, slots * fields, block), F32),
            pltpu.VMEM((devices, slots * fields, block), F32),
            pltpu.VMEM((devices, slots, 1, block), jnp.int32),
            pltpu.VMEM((devices, slots, 1, block), jnp.int32),
            pltpu.VMEM((planes + 2 * levels, tall, cols), F32),
            pltpu.VMEM((tall, cols), F32),
        ]
        + [pltpu.VMEM((pairs + 1, 8, cols), F32)] * 4
        + [pltpu.VMEM((groups, tall, cols), F32)]
        + [pltpu.VMEM((groups // 2 + 1, tall, cols), F32)] * 4
        + [
            pltpu.VMEM((2, groups, tall, cols), F32),
            pltpu.VMEM((NSUB, tracer_count, tall, cols), F32),
            pltpu.VMEM((3, tall, cols), F32),
            dma((8,)),
            dma((devices,)),
            dma((devices,)),
            dma((devices,)),
            dma((devices,)),
            dma((devices,)),
            dma((2,)),
            dma((2,)),
            dma((2,)),
            dma((2,)),
        ],
        compiler_params=pltpu.CompilerParams(
            collective_id=0, has_side_effects=True, vmem_limit_bytes=60 * 1024 * 1024
        ),
    )(
        source_block,
        target_block,
        block_count,
        atm_fluxes,
        remap_weights.reshape(devices * slots, block, block),
        tracers.reshape(planes, rows, cols),
        east_velocity,
        north_velocity,
        land_mask,
    )
    out = pl.pallas_call(
        couple_kernel,
        out_shape=shape((planes, rows, cols), F32),
        in_specs=[anywhere] * 4,
        out_specs=anywhere,
        scratch_shapes=[
            pltpu.VMEM((rows, fields, block), F32),
            pltpu.VMEM((rows, cols), jnp.int32),
            pltpu.VMEM((fields, planes), F32),
            pltpu.VMEM((planes, rows, cols), F32),
            pltpu.VMEM((rows * planes, cols), F32),
            pltpu.VMEM((planes, rows, cols), F32),
            dma((4,)),
            dma((tracer_count,)),
        ],
        compiler_params=pltpu.CompilerParams(vmem_limit_bytes=60 * 1024 * 1024),
    )(flux, land_mask, coupling.T, advected)
    return out.reshape(tracers.shape)


def solution(mesh):
    placed = (
        P(None, ("lat", "lon")),
        P(("lat", "lon"), None, None, None),
        P(("lat", "lon"), None),
        P(("lat", "lon"), None),
        P(("lat", "lon"), None),
        P(None, None, "lat", "lon"),
        P(None, "lat", "lon"),
        P(None, "lat", "lon"),
        P("lat", "lon"),
        P(),
    )
    return jax.shard_map(
        functools.partial(per_device, mesh.shape["lat"], mesh.shape["lon"]),
        mesh=mesh,
        in_specs=placed,
        out_specs=P(None, None, "lat", "lon"),
        check_vma=False,
    )
```

```python
import functools

import jax
import jax.numpy as jnp
from jax import lax
from jax.experimental import pallas as pl
from jax.experimental.pallas import tpu as pltpu
from jax.sharding import PartitionSpec as P

NSUB = 4
DIFFUSION = 0.2
MESH = pl.DeviceIdType.MESH
F32 = jnp.float32


def offsets(step, n_lat, n_lon):
    ring = lax.rem(step, n_lon)
    hop = (ring + 1) // 2
    d_lon = lax.rem(n_lon // 2 + jnp.where(ring % 2 == 1, -hop, hop) + n_lon, n_lon)
    d_lat = lax.rem(step // n_lon + 1, n_lat)
    return d_lat, d_lon


def shifted(field):
    cols, rows = field.shape[1], field.shape[0]
    return (
        pltpu.roll(field, cols - 1, 1),
        pltpu.roll(field, 1, 1),
        pltpu.roll(field, rows - 1, 0),
        pltpu.roll(field, 1, 0),
    )


def faces(east, north, sea):
    sea_east = sea * pltpu.roll(sea, sea.shape[1] - 1, 1)
    sea_north = sea * pltpu.roll(sea, sea.shape[0] - 1, 0)
    return (
        sea_east * (0.5 * east + DIFFUSION),
        sea_east * (0.5 * east - DIFFUSION),
        sea_north * (0.5 * north + DIFFUSION),
        sea_north * (0.5 * north - DIFFUSION),
    )


def exchange_kernel(
    n_lat,
    n_lon,
    source_hbm,
    target_hbm,
    count_hbm,
    atm_hbm,
    weights_hbm,
    tracers_hbm,
    east_hbm,
    north_hbm,
    land_hbm,
    flux_ref,
    advected_hbm,
    source_ref,
    target_ref,
    count_ref,
    atm_ref,
    land_ref,
    advected_ref,
    atm_blocks,
    weights,
    parts,
    arrived,
    marks,
    landed,
    state,
    sea,
    to_north,
    to_south,
    from_north,
    from_south,
    edge,
    to_east,
    to_west,
    from_east,
    from_west,
    strip,
    beyond,
    sides,
    load_sem,
    weight_sem,
    part_send,
    part_recv,
    mark_send,
    mark_recv,
    lat_send,
    lat_recv,
    lon_send,
    lon_recv,
):
    lat, lon = lax.axis_index("lat"), lax.axis_index("lon")
    me = lat * n_lon + lon
    devices = n_lat * n_lon
    fields, block = atm_blocks.shape[1:]
    slots = marks.shape[1]
    planes, rows, cols = tracers_hbm.shape
    levels = east_hbm.shape[0]
    tracer_count = planes // levels
    total = planes + 2 * levels
    pairs = total // 2

    def partner(step):
        d_lat, d_lon = offsets(step, n_lat, n_lon)
        return lax.rem(lat + d_lat, n_lat), lax.rem(lon + d_lon, n_lon)

    def origin(step):
        d_lat, d_lon = offsets(step, n_lat, n_lon)
        return lax.rem(lat - d_lat + n_lat, n_lat) * n_lon + lax.rem(lon - d_lon + n_lon, n_lon)

    barrier = pltpu.get_barrier_semaphore()

    @pl.loop(0, devices - 1)
    def _(step):
        pl.semaphore_signal(barrier, inc=1, device_id=partner(step), device_id_type=MESH)

    inner = pl.ds(0, rows)
    loads = [
        pltpu.make_async_copy(a, b, load_sem.at[n])
        for n, (a, b) in enumerate(
            (
                (tracers_hbm, state.at[pl.ds(0, planes), inner, :]),
                (east_hbm, state.at[pl.ds(planes, levels), inner, :]),
                (north_hbm, state.at[pl.ds(planes + levels, levels), inner, :]),
                (land_hbm, land_ref),
                (source_hbm, source_ref),
                (target_hbm, target_ref),
                (count_hbm, count_ref),
                (atm_hbm, atm_ref),
            )
        )
    ]
    for load in loads:
        load.start()

    def weight_copy(step):
        p_lat, p_lon = partner(step)
        tile = p_lat * n_lon + p_lon
        return pltpu.make_async_copy(
            weights_hbm.at[pl.ds(tile * slots, slots)],
            weights.at[pl.ds(step * slots, slots)],
            weight_sem.at[step],
        )

    @pl.loop(0, devices)
    def _(step):
        weight_copy(step).start()

    for load in loads[:4]:
        load.wait()
    sea[0:rows, :] = land_ref[...].astype(F32)

    upper = lax.broadcasted_iota(jnp.int32, (8, cols), 0) < 4

    @pl.loop(0, pairs)
    def _(i):
        low, high = state[i, 0:8, :], state[i + pairs, 0:8, :]
        to_south[i] = jnp.where(upper, low, pltpu.roll(high, 4, 0))
        low, high = state[i, rows - 8 : rows, :], state[i + pairs, rows - 8 : rows, :]
        to_north[i] = jnp.where(upper, pltpu.roll(high, 4, 0), low)

    to_south[pairs] = sea[0:8, :]
    to_north[pairs] = sea[rows - 8 : rows, :]
    pl.semaphore_wait(barrier, devices - 1)

    def lat_copy(north):
        ref, into, to, way = (
            (to_north, from_south, lat + 1, 0) if north else (to_south, from_north, lat - 1, 1)
        )
        return pltpu.make_async_remote_copy(
            src_ref=ref,
            dst_ref=into,
            send_sem=lat_send.at[way],
            recv_sem=lat_recv.at[way],
            device_id=(to, lon),
            device_id_type=MESH,
        )

    @pl.when(lat < n_lat - 1)
    def _():
        lat_copy(True).start()

    @pl.when(lat > 0)
    def _():
        lat_copy(False).start()

    for load in loads[4:]:
        load.wait()
    for b in range(atm_blocks.shape[0]):
        atm_blocks[b] = atm_ref[:, b * block : (b + 1) * block].astype(F32)

    def mark_copy(step):
        return pltpu.make_async_remote_copy(
            src_ref=marks.at[step],
            dst_ref=landed.at[me],
            send_sem=mark_send.at[step],
            recv_sem=mark_recv.at[step],
            device_id=partner(step),
            device_id_type=MESH,
        )

    def part_copy(step):
        return pltpu.make_async_remote_copy(
            src_ref=parts.at[step],
            dst_ref=arrived.at[me],
            send_sem=part_send.at[step],
            recv_sem=part_recv.at[step],
            device_id=partner(step),
            device_id_type=MESH,
        )

    def remap(step, into, at):
        p_lat, p_lon = partner(step)
        tile = p_lat * n_lon + p_lon
        weight_copy(step).wait()
        for k in range(slots):
            mark = jnp.where(k < count_ref[0, tile], target_ref[0, tile * slots + k], -1)
            marks[step, k] = jnp.full((1, block), mark, jnp.int32)
            chosen = atm_blocks[source_ref[0, tile * slots + k]].astype(jnp.bfloat16)
            into[at, k * fields : (k + 1) * fields, :] = jnp.dot(
                chosen, weights[step * slots + k], preferred_element_type=F32
            )

    def send(step):
        remap(step, parts, step)
        mark_copy(step).start()
        part_copy(step).start()

    early = devices // 8
    pl.loop(0, early)(send)

    @pl.when(lat > 0)
    def _():
        lat_copy(True).wait_recv()

    @pl.when(lat < n_lat - 1)
    def _():
        lat_copy(False).wait_recv()

    @pl.when(lat == 0)
    def _():
        from_south[...] = jnp.zeros_like(from_south)

    @pl.when(lat == n_lat - 1)
    def _():
        from_north[...] = jnp.zeros_like(from_north)

    @pl.loop(0, pairs)
    def _(i):
        north, south = from_north[i], from_south[i]
        state[i, rows:, :] = jnp.where(upper, north, south)
        state[i + pairs, rows:, :] = pltpu.roll(jnp.where(upper, south, north), 4, 0)

    sea[rows:, :] = jnp.where(upper, from_north[pairs], from_south[pairs])

    width = cols // levels
    near = width // 2
    groups = tracer_count + 3
    joint = groups // 2
    lane = lax.broadcasted_iota(jnp.int32, (rows + 8, cols), 1)
    place = lax.rem(lane, width)
    west_side = place < near
    edge[...] = jnp.zeros_like(edge)

    @pl.loop(0, levels)
    def _(level):
        here = (lane >= level * width) & (lane < (level + 1) * width)
        shift = level * width + near
        for group in range(groups):
            field = state[group * levels + level] if group < groups - 1 else sea[...]
            edge[group] = jnp.where(here, pltpu.roll(field, shift, 1), edge[group])

    for group in range(joint):
        low, high = edge[group], edge[group + joint]
        to_east[group] = jnp.where(west_side, low, pltpu.roll(high, near, 1))
        to_west[group] = jnp.where(west_side, pltpu.roll(high, cols - near, 1), low)
    to_east[joint] = edge[groups - 1]
    to_west[joint] = edge[groups - 1]

    def lon_copy(east):
        ref, into, to, way = (
            (to_east, from_west, lon + 1, 0) if east else (to_west, from_east, lon + n_lon - 1, 1)
        )
        return pltpu.make_async_remote_copy(
            src_ref=ref,
            dst_ref=into,
            send_sem=lon_send.at[way],
            recv_sem=lon_recv.at[way],
            device_id=(lat, lax.rem(to, n_lon)),
            device_id_type=MESH,
        )

    lon_copy(True).start()
    lon_copy(False).start()

    pl.loop(early, devices - 1)(send)
    remap(devices - 1, arrived, me)
    landed[me] = marks[devices - 1]

    flux_ref[...] = jnp.zeros_like(flux_ref)

    def gather(source):
        seen = [jnp.broadcast_to(landed[source, k], (8, block)) for k in range(slots)]
        for first in range(0, fields, 8):
            part = [
                arrived[source, k * fields + first : k * fields + first + 8, :]
                for k in range(slots)
            ]
            for row in range(rows):
                added = flux_ref[row, first : first + 8, :]
                for k in range(slots):
                    added = added + jnp.where(seen[k] == row, part[k], 0.0)
                flux_ref[row, first : first + 8, :] = added

    gather(me)

    lon_copy(True).wait_recv()
    lon_copy(False).wait_recv()
    for group in range(joint):
        low, high = edge[group], edge[group + joint]
        east, west = from_east[group], from_west[group]
        strip[0, group] = jnp.where(west_side, low, east)
        strip[0, group + joint] = jnp.where(west_side, high, pltpu.roll(east, near, 1))
        strip[1, group] = jnp.where(west_side, west, low)
        strip[1, group + joint] = jnp.where(west_side, pltpu.roll(west, cols - near, 1), high)
    strip[0, groups - 1] = jnp.where(west_side, edge[groups - 1], from_east[joint])
    strip[1, groups - 1] = jnp.where(west_side, from_west[joint], edge[groups - 1])

    stencils = []
    for side in range(2):
        sea_strip = strip[side, groups - 1]
        a, b, c, d = faces(strip[side, tracer_count], strip[side, tracer_count + 1], sea_strip)
        a_west, b_west = pltpu.roll(a, 1, 1), pltpu.roll(b, 1, 1)
        c_south, d_south = pltpu.roll(c, 1, 0), pltpu.roll(d, 1, 0)
        stencils.append((1.0 - a + b_west - c + d_south, -b, a_west, -d, c_south))
        if side == 1:
            sides[0] = a_west
            sides[1] = b_west
        else:
            sides[2] = pltpu.roll(sea_strip, cols - 1, 1)

    @pl.loop(0, tracer_count)
    def _(t):
        now = [strip[0, t], strip[1, t]]
        for step in range(NSUB):
            east_of = pltpu.roll(now[0], cols - 1, 1)
            west_of = pltpu.roll(now[1], 1, 1)
            beyond[step, t] = jnp.where(west_side, east_of, west_of)
            if step < NSUB - 1:
                for side in range(2):
                    own, e, w, n, s = stencils[side]
                    qe, qw, qn, qs = shifted(now[side])
                    now[side] = own * now[side] + e * qe + w * qw + n * qn + s * qs

    first_lane, last_lane = lane == 0, lane == cols - 1
    sea_all = sea[...]

    @pl.loop(0, levels)
    def _(level):
        shift = lax.rem(2 * cols - level * width - near, cols)
        east, north = state[planes + level], state[planes + levels + level]
        sea_beyond = pltpu.roll(sides[2], shift, 1)
        sea_east = sea_all * jnp.where(last_lane, sea_beyond, pltpu.roll(sea_all, cols - 1, 1))
        _, _, c, d = faces(east, north, sea_all)
        a = sea_east * (0.5 * east + DIFFUSION)
        b = sea_east * (0.5 * east - DIFFUSION)
        a_west = jnp.where(first_lane, pltpu.roll(sides[0], shift, 1), pltpu.roll(a, 1, 1))
        b_west = jnp.where(first_lane, pltpu.roll(sides[1], shift, 1), pltpu.roll(b, 1, 1))
        c_south, d_south = pltpu.roll(c, 1, 0), pltpu.roll(d, 1, 0)
        own = 1.0 - a + b_west - c + d_south
        for t in range(tracer_count):
            now = state[t * levels + level]
            for step in range(NSUB):
                outer = pltpu.roll(beyond[step, t], shift, 1)
                qe, qw, qn, qs = shifted(now)
                qe, qw = jnp.where(last_lane, outer, qe), jnp.where(first_lane, outer, qw)
                now = own * now - b * qe + a_west * qw - d * qn + c_south * qs
            advected_ref[t * levels + level] = now[:rows]

    saved = pltpu.make_async_copy(advected_ref, advected_hbm, load_sem.at[0])
    saved.start()

    @pl.loop(0, devices - 1)
    def _(step):
        mark_copy(step).wait_recv()
        pltpu.make_async_remote_copy(
            src_ref=parts.at[step],
            dst_ref=arrived.at[origin(step)],
            send_sem=part_send.at[step],
            recv_sem=part_recv.at[step],
            device_id=partner(step),
            device_id_type=MESH,
        ).wait_recv()
        gather(origin(step))

    @pl.loop(0, devices - 1)
    def _(step):
        mark_copy(step).wait_send()
        part_copy(step).wait_send()

    @pl.when(lat < n_lat - 1)
    def _():
        lat_copy(True).wait_send()

    @pl.when(lat > 0)
    def _():
        lat_copy(False).wait_send()

    lon_copy(True).wait_send()
    lon_copy(False).wait_send()
    saved.wait()


def couple_kernel(
    flux_hbm,
    land_hbm,
    coupling_hbm,
    advected_hbm,
    out_ref,
    flux_ref,
    land_ref,
    coupling_ref,
    advected_ref,
    source,
    result,
    load_sem,
    sem,
):
    rows, cols = land_ref.shape
    planes = advected_ref.shape[0]
    pieces = sem.shape[0]
    share = planes // pieces
    loads = [
        pltpu.make_async_copy(a, b, load_sem.at[n])
        for n, (a, b) in enumerate(
            (
                (flux_hbm, flux_ref),
                (land_hbm, land_ref),
                (coupling_hbm, coupling_ref),
                (advected_hbm, advected_ref),
            )
        )
    ]
    for load in loads:
        load.start()
    for load in loads[:3]:
        load.wait()
    coupling = coupling_ref[...]
    lead = coupling.astype(jnp.bfloat16).astype(F32)
    factors = jnp.concatenate([lead, lead, coupling - lead], axis=0).astype(jnp.bfloat16)
    for row in range(rows):
        flux = flux_ref[row]
        head = flux.astype(jnp.bfloat16).astype(F32)
        stack = jnp.concatenate([head, flux - head, head], axis=0).astype(jnp.bfloat16)
        source[row * planes : (row + 1) * planes, :] = lax.dot_general(
            factors, stack, (((0,), (0,)), ((), ())), preferred_element_type=F32
        )
    sea = land_ref[...].astype(F32)
    loads[3].wait()
    copies = []
    for piece in range(pieces):
        for plane in range(piece * share, (piece + 1) * share):
            added = source[pl.ds(plane, rows, planes), :]
            result[plane] = advected_ref[plane] + sea * added
        here = pl.ds(piece * share, share)
        copies.append(pltpu.make_async_copy(result.at[here], out_ref.at[here], sem.at[piece]))
        copies[-1].start()
    for copy in copies:
        copy.wait()


def per_device(
    n_lat,
    n_lon,
    atm_fluxes,
    remap_weights,
    source_block,
    target_block,
    block_count,
    tracers,
    east_velocity,
    north_velocity,
    land_mask,
    coupling,
):
    fields, cells = atm_fluxes.shape
    block = remap_weights.shape[-1]
    devices = n_lat * n_lon
    slots = source_block.shape[1] // devices
    tracer_count, levels, rows, cols = tracers.shape
    planes = tracer_count * levels
    groups = tracer_count + 3
    tall = rows + 8
    pairs = planes // 2 + levels
    vmem = pl.BlockSpec(memory_space=pltpu.VMEM)
    anywhere = pl.BlockSpec(memory_space=pl.ANY)
    dma = pltpu.SemaphoreType.DMA
    shape = jax.ShapeDtypeStruct
    flux, advected = pl.pallas_call(
        functools.partial(exchange_kernel, n_lat, n_lon),
        out_shape=(
            shape((rows, fields, block), F32),
            shape((planes, rows, cols), F32),
        ),
        in_specs=[anywhere] * 9,
        out_specs=(vmem, anywhere),
        scratch_shapes=[
            pltpu.SMEM(source_block.shape, jnp.int32),
            pltpu.SMEM(target_block.shape, jnp.int32),
            pltpu.SMEM(block_count.shape, jnp.int32),
            pltpu.VMEM((fields, cells), jnp.bfloat16),
            pltpu.VMEM((rows, cols), jnp.int32),
            pltpu.VMEM((planes, rows, cols), F32),
            pltpu.VMEM((cells // block, fields, block), F32),
            pltpu.VMEM((devices * slots, block, block), jnp.bfloat16),
            pltpu.VMEM((devices, slots * fields, block), F32),
            pltpu.VMEM((devices, slots * fields, block), F32),
            pltpu.VMEM((devices, slots, 1, block), jnp.int32),
            pltpu.VMEM((devices, slots, 1, block), jnp.int32),
            pltpu.VMEM((planes + 2 * levels, tall, cols), F32),
            pltpu.VMEM((tall, cols), F32),
        ]
        + [pltpu.VMEM((pairs + 1, 8, cols), F32)] * 4
        + [pltpu.VMEM((groups, tall, cols), F32)]
        + [pltpu.VMEM((groups // 2 + 1, tall, cols), F32)] * 4
        + [
            pltpu.VMEM((2, groups, tall, cols), F32),
            pltpu.VMEM((NSUB, tracer_count, tall, cols), F32),
            pltpu.VMEM((3, tall, cols), F32),
            dma((8,)),
            dma((devices,)),
            dma((devices,)),
            dma((devices,)),
            dma((devices,)),
            dma((devices,)),
            dma((2,)),
            dma((2,)),
            dma((2,)),
            dma((2,)),
        ],
        compiler_params=pltpu.CompilerParams(
            collective_id=0, has_side_effects=True, vmem_limit_bytes=60 * 1024 * 1024
        ),
    )(
        source_block,
        target_block,
        block_count,
        atm_fluxes,
        remap_weights.reshape(devices * slots, block, block),
        tracers.reshape(planes, rows, cols),
        east_velocity,
        north_velocity,
        land_mask,
    )
    out = pl.pallas_call(
        couple_kernel,
        out_shape=shape((planes, rows, cols), F32),
        in_specs=[anywhere] * 4,
        out_specs=anywhere,
        scratch_shapes=[
            pltpu.VMEM((rows, fields, block), F32),
            pltpu.VMEM((rows, cols), jnp.int32),
            pltpu.VMEM((fields, planes), F32),
            pltpu.VMEM((planes, rows, cols), F32),
            pltpu.VMEM((rows * planes, cols), F32),
            pltpu.VMEM((planes, rows, cols), F32),
            dma((4,)),
            dma((tracer_count,)),
        ],
        compiler_params=pltpu.CompilerParams(vmem_limit_bytes=60 * 1024 * 1024),
    )(flux, land_mask, coupling.T, advected)
    return out.reshape(tracers.shape)


def solution(mesh):
    placed = (
        P(None, ("lat", "lon")),
        P(("lat", "lon"), None, None, None),
        P(("lat", "lon"), None),
        P(("lat", "lon"), None),
        P(("lat", "lon"), None),
        P(None, None, "lat", "lon"),
        P(None, "lat", "lon"),
        P(None, "lat", "lon"),
        P("lat", "lon"),
        P(),
    )
    return jax.shard_map(
        functools.partial(per_device, mesh.shape["lat"], mesh.shape["lon"]),
        mesh=mesh,
        in_specs=placed,
        out_specs=P(None, None, "lat", "lon"),
        check_vma=False,
    )
```

```python
import functools

import jax
import jax.numpy as jnp
from jax import lax
from jax.experimental import pallas as pl
from jax.experimental.pallas import tpu as pltpu
from jax.sharding import PartitionSpec as P

NSUB = 4
DIFFUSION = 0.2
MESH = pl.DeviceIdType.MESH
F32 = jnp.float32


def offsets(step, n_lat, n_lon):
    ring = lax.rem(step, n_lon)
    hop = (ring + 1) // 2
    d_lon = lax.rem(n_lon // 2 + jnp.where(ring % 2 == 1, -hop, hop) + n_lon, n_lon)
    d_lat = lax.rem(step // n_lon + 1, n_lat)
    return d_lat, d_lon


def shifted(field):
    cols, rows = field.shape[1], field.shape[0]
    return (
        pltpu.roll(field, cols - 1, 1),
        pltpu.roll(field, 1, 1),
        pltpu.roll(field, rows - 1, 0),
        pltpu.roll(field, 1, 0),
    )


def faces(east, north, sea):
    sea_east = sea * pltpu.roll(sea, sea.shape[1] - 1, 1)
    sea_north = sea * pltpu.roll(sea, sea.shape[0] - 1, 0)
    return (
        sea_east * (0.5 * east + DIFFUSION),
        sea_east * (0.5 * east - DIFFUSION),
        sea_north * (0.5 * north + DIFFUSION),
        sea_north * (0.5 * north - DIFFUSION),
    )


def exchange_kernel(
    n_lat,
    n_lon,
    source_hbm,
    target_hbm,
    count_hbm,
    atm_hbm,
    weights_hbm,
    tracers_hbm,
    east_hbm,
    north_hbm,
    land_hbm,
    flux_ref,
    advected_hbm,
    source_ref,
    target_ref,
    count_ref,
    atm_ref,
    land_ref,
    advected_ref,
    atm_blocks,
    weights,
    parts,
    arrived,
    marks,
    landed,
    state,
    sea,
    to_north,
    to_south,
    from_north,
    from_south,
    edge,
    to_east,
    to_west,
    from_east,
    from_west,
    strip,
    beyond,
    sides,
    load_sem,
    weight_sem,
    part_send,
    part_recv,
    mark_send,
    mark_recv,
    lat_send,
    lat_recv,
    lon_send,
    lon_recv,
):
    lat, lon = lax.axis_index("lat"), lax.axis_index("lon")
    me = lat * n_lon + lon
    devices = n_lat * n_lon
    fields, block = atm_blocks.shape[1:]
    slots = marks.shape[1]
    planes, rows, cols = tracers_hbm.shape
    levels = east_hbm.shape[0]
    tracer_count = planes // levels
    total = planes + 2 * levels
    pairs = total // 2

    def partner(step):
        d_lat, d_lon = offsets(step, n_lat, n_lon)
        return lax.rem(lat + d_lat, n_lat), lax.rem(lon + d_lon, n_lon)

    def origin(step):
        d_lat, d_lon = offsets(step, n_lat, n_lon)
        return lax.rem(lat - d_lat + n_lat, n_lat) * n_lon + lax.rem(lon - d_lon + n_lon, n_lon)

    barrier = pltpu.get_barrier_semaphore()

    @pl.loop(0, devices - 1)
    def _(step):
        pl.semaphore_signal(barrier, inc=1, device_id=partner(step), device_id_type=MESH)

    inner = pl.ds(0, rows)
    loads = [
        pltpu.make_async_copy(a, b, load_sem.at[n])
        for n, (a, b) in enumerate(
            (
                (tracers_hbm, state.at[pl.ds(0, planes), inner, :]),
                (east_hbm, state.at[pl.ds(planes, levels), inner, :]),
                (north_hbm, state.at[pl.ds(planes + levels, levels), inner, :]),
                (land_hbm, land_ref),
                (source_hbm, source_ref),
                (target_hbm, target_ref),
                (count_hbm, count_ref),
                (atm_hbm, atm_ref),
            )
        )
    ]
    for load in loads:
        load.start()

    def weight_copy(step):
        p_lat, p_lon = partner(step)
        tile = p_lat * n_lon + p_lon
        return pltpu.make_async_copy(
            weights_hbm.at[pl.ds(tile * slots, slots)],
            weights.at[pl.ds(step * slots, slots)],
            weight_sem.at[step],
        )

    @pl.loop(0, devices)
    def _(step):
        weight_copy(step).start()

    for load in loads[:4]:
        load.wait()
    sea[0:rows, :] = land_ref[...].astype(F32)

    upper = lax.broadcasted_iota(jnp.int32, (8, cols), 0) < 4

    @pl.loop(0, pairs)
    def _(i):
        low, high = state[i, 0:8, :], state[i + pairs, 0:8, :]
        to_south[i] = jnp.where(upper, low, pltpu.roll(high, 4, 0))
        low, high = state[i, rows - 8 : rows, :], state[i + pairs, rows - 8 : rows, :]
        to_north[i] = jnp.where(upper, pltpu.roll(high, 4, 0), low)

    to_south[pairs] = sea[0:8, :]
    to_north[pairs] = sea[rows - 8 : rows, :]
    pl.semaphore_wait(barrier, devices - 1)

    def lat_copy(north):
        ref, into, to, way = (
            (to_north, from_south, lat + 1, 0) if north else (to_south, from_north, lat - 1, 1)
        )
        return pltpu.make_async_remote_copy(
            src_ref=ref,
            dst_ref=into,
            send_sem=lat_send.at[way],
            recv_sem=lat_recv.at[way],
            device_id=(to, lon),
            device_id_type=MESH,
        )

    @pl.when(lat < n_lat - 1)
    def _():
        lat_copy(True).start()

    @pl.when(lat > 0)
    def _():
        lat_copy(False).start()

    for load in loads[4:]:
        load.wait()
    for b in range(atm_blocks.shape[0]):
        atm_blocks[b] = atm_ref[:, b * block : (b + 1) * block].astype(F32)

    def mark_copy(step):
        return pltpu.make_async_remote_copy(
            src_ref=marks.at[step],
            dst_ref=landed.at[me],
            send_sem=mark_send.at[step],
            recv_sem=mark_recv.at[step],
            device_id=partner(step),
            device_id_type=MESH,
        )

    def part_copy(step):
        return pltpu.make_async_remote_copy(
            src_ref=parts.at[step],
            dst_ref=arrived.at[me],
            send_sem=part_send.at[step],
            recv_sem=part_recv.at[step],
            device_id=partner(step),
            device_id_type=MESH,
        )

    def remap(step, into, at):
        p_lat, p_lon = partner(step)
        tile = p_lat * n_lon + p_lon
        for k in range(slots):
            mark = jnp.where(k < count_ref[0, tile], target_ref[0, tile * slots + k], -1)
            marks[step, k] = jnp.full((1, block), mark, jnp.int32)
            chosen = atm_blocks[source_ref[0, tile * slots + k]].astype(jnp.bfloat16)
            into[at, k * fields : (k + 1) * fields, :] = jnp.dot(
                chosen, weights[step * slots + k], preferred_element_type=F32
            )

    def send(first, count):
        steps = [first + n for n in range(count)]
        for step in steps:
            weight_copy(step).wait()
        for step in steps:
            remap(step, parts, step)
        for step in steps:
            mark_copy(step).start()
            part_copy(step).start()

    early = devices // 8 + 1
    assert (devices - 1 - early) % 2 == 0
    pl.loop(0, early)(lambda step: send(step, 1))

    @pl.when(lat > 0)
    def _():
        lat_copy(True).wait_recv()

    @pl.when(lat < n_lat - 1)
    def _():
        lat_copy(False).wait_recv()

    @pl.when(lat == 0)
    def _():
        from_south[...] = jnp.zeros_like(from_south)

    @pl.when(lat == n_lat - 1)
    def _():
        from_north[...] = jnp.zeros_like(from_north)

    @pl.loop(0, pairs)
    def _(i):
        north, south = from_north[i], from_south[i]
        state[i, rows:, :] = jnp.where(upper, north, south)
        state[i + pairs, rows:, :] = pltpu.roll(jnp.where(upper, south, north), 4, 0)

    sea[rows:, :] = jnp.where(upper, from_north[pairs], from_south[pairs])

    width = cols // levels
    near = width // 2
    groups = tracer_count + 3
    joint = groups // 2
    lane = lax.broadcasted_iota(jnp.int32, (rows + 8, cols), 1)
    place = lax.rem(lane, width)
    west_side = place < near
    edge[...] = jnp.zeros_like(edge)

    @pl.loop(0, levels)
    def _(level):
        here = (lane >= level * width) & (lane < (level + 1) * width)
        shift = level * width + near
        for group in range(groups):
            field = state[group * levels + level] if group < groups - 1 else sea[...]
            edge[group] = jnp.where(here, pltpu.roll(field, shift, 1), edge[group])

    for group in range(joint):
        low, high = edge[group], edge[group + joint]
        to_east[group] = jnp.where(west_side, low, pltpu.roll(high, near, 1))
        to_west[group] = jnp.where(west_side, pltpu.roll(high, cols - near, 1), low)
    to_east[joint] = edge[groups - 1]
    to_west[joint] = edge[groups - 1]

    def lon_copy(east):
        ref, into, to, way = (
            (to_east, from_west, lon + 1, 0) if east else (to_west, from_east, lon + n_lon - 1, 1)
        )
        return pltpu.make_async_remote_copy(
            src_ref=ref,
            dst_ref=into,
            send_sem=lon_send.at[way],
            recv_sem=lon_recv.at[way],
            device_id=(lat, lax.rem(to, n_lon)),
            device_id_type=MESH,
        )

    lon_copy(True).start()
    lon_copy(False).start()

    pl.loop(0, (devices - 1 - early) // 2)(lambda pair: send(early + 2 * pair, 2))
    weight_copy(devices - 1).wait()
    remap(devices - 1, arrived, me)
    landed[me] = marks[devices - 1]

    flux_ref[...] = jnp.zeros_like(flux_ref)

    def gather(source):
        seen = [jnp.broadcast_to(landed[source, k], (8, block)) for k in range(slots)]
        for first in range(0, fields, 8):
            part = [
                arrived[source, k * fields + first : k * fields + first + 8, :]
                for k in range(slots)
            ]
            for row in range(rows):
                added = flux_ref[row, first : first + 8, :]
                for k in range(slots):
                    added = added + jnp.where(seen[k] == row, part[k], 0.0)
                flux_ref[row, first : first + 8, :] = added

    gather(me)

    lon_copy(True).wait_recv()
    lon_copy(False).wait_recv()
    for group in range(joint):
        low, high = edge[group], edge[group + joint]
        east, west = from_east[group], from_west[group]
        strip[0, group] = jnp.where(west_side, low, east)
        strip[0, group + joint] = jnp.where(west_side, high, pltpu.roll(east, near, 1))
        strip[1, group] = jnp.where(west_side, west, low)
        strip[1, group + joint] = jnp.where(west_side, pltpu.roll(west, cols - near, 1), high)
    strip[0, groups - 1] = jnp.where(west_side, edge[groups - 1], from_east[joint])
    strip[1, groups - 1] = jnp.where(west_side, from_west[joint], edge[groups - 1])

    stencils = []
    for side in range(2):
        sea_strip = strip[side, groups - 1]
        a, b, c, d = faces(strip[side, tracer_count], strip[side, tracer_count + 1], sea_strip)
        a_west, b_west = pltpu.roll(a, 1, 1), pltpu.roll(b, 1, 1)
        c_south, d_south = pltpu.roll(c, 1, 0), pltpu.roll(d, 1, 0)
        stencils.append((1.0 - a + b_west - c + d_south, -b, a_west, -d, c_south))
        if side == 1:
            sides[0] = a_west
            sides[1] = b_west
        else:
            sides[2] = pltpu.roll(sea_strip, cols - 1, 1)

    @pl.loop(0, tracer_count)
    def _(t):
        now = [strip[0, t], strip[1, t]]
        for step in range(NSUB):
            east_of = pltpu.roll(now[0], cols - 1, 1)
            west_of = pltpu.roll(now[1], 1, 1)
            beyond[step, t] = jnp.where(west_side, east_of, west_of)
            if step < NSUB - 1:
                for side in range(2):
                    own, e, w, n, s = stencils[side]
                    qe, qw, qn, qs = shifted(now[side])
                    now[side] = own * now[side] + e * qe + w * qw + n * qn + s * qs

    first_lane, last_lane = lane == 0, lane == cols - 1
    sea_all = sea[...]

    @pl.loop(0, levels)
    def _(level):
        shift = lax.rem(2 * cols - level * width - near, cols)
        east, north = state[planes + level], state[planes + levels + level]
        sea_beyond = pltpu.roll(sides[2], shift, 1)
        sea_east = sea_all * jnp.where(last_lane, sea_beyond, pltpu.roll(sea_all, cols - 1, 1))
        _, _, c, d = faces(east, north, sea_all)
        a = sea_east * (0.5 * east + DIFFUSION)
        b = sea_east * (0.5 * east - DIFFUSION)
        a_west = jnp.where(first_lane, pltpu.roll(sides[0], shift, 1), pltpu.roll(a, 1, 1))
        b_west = jnp.where(first_lane, pltpu.roll(sides[1], shift, 1), pltpu.roll(b, 1, 1))
        c_south, d_south = pltpu.roll(c, 1, 0), pltpu.roll(d, 1, 0)
        own = 1.0 - a + b_west - c + d_south
        for t in range(tracer_count):
            now = state[t * levels + level]
            for step in range(NSUB):
                outer = pltpu.roll(beyond[step, t], shift, 1)
                qe, qw, qn, qs = shifted(now)
                qe, qw = jnp.where(last_lane, outer, qe), jnp.where(first_lane, outer, qw)
                now = own * now - b * qe + a_west * qw - d * qn + c_south * qs
            advected_ref[t * levels + level] = now[:rows]

    saved = pltpu.make_async_copy(advected_ref, advected_hbm, load_sem.at[0])
    saved.start()

    @pl.loop(0, devices - 1)
    def _(step):
        mark_copy(step).wait_recv()
        pltpu.make_async_remote_copy(
            src_ref=parts.at[step],
            dst_ref=arrived.at[origin(step)],
            send_sem=part_send.at[step],
            recv_sem=part_recv.at[step],
            device_id=partner(step),
            device_id_type=MESH,
        ).wait_recv()
        gather(origin(step))

    @pl.loop(0, devices - 1)
    def _(step):
        mark_copy(step).wait_send()
        part_copy(step).wait_send()

    @pl.when(lat < n_lat - 1)
    def _():
        lat_copy(True).wait_send()

    @pl.when(lat > 0)
    def _():
        lat_copy(False).wait_send()

    lon_copy(True).wait_send()
    lon_copy(False).wait_send()
    saved.wait()


def couple_kernel(
    flux_hbm,
    land_hbm,
    coupling_hbm,
    advected_hbm,
    out_ref,
    flux_ref,
    land_ref,
    coupling_ref,
    advected_ref,
    source,
    result,
    load_sem,
    sem,
):
    rows, cols = land_ref.shape
    planes = advected_ref.shape[0]
    pieces = sem.shape[0]
    share = planes // pieces
    loads = [
        pltpu.make_async_copy(a, b, load_sem.at[n])
        for n, (a, b) in enumerate(
            (
                (flux_hbm, flux_ref),
                (land_hbm, land_ref),
                (coupling_hbm, coupling_ref),
                (advected_hbm, advected_ref),
            )
        )
    ]
    for load in loads:
        load.start()
    for load in loads[:3]:
        load.wait()
    coupling = coupling_ref[...]
    lead = coupling.astype(jnp.bfloat16).astype(F32)
    factors = jnp.concatenate([lead, lead, coupling - lead], axis=0).astype(jnp.bfloat16)
    for row in range(rows):
        flux = flux_ref[row]
        head = flux.astype(jnp.bfloat16).astype(F32)
        stack = jnp.concatenate([head, flux - head, head], axis=0).astype(jnp.bfloat16)
        source[row * planes : (row + 1) * planes, :] = lax.dot_general(
            factors, stack, (((0,), (0,)), ((), ())), preferred_element_type=F32
        )
    sea = land_ref[...].astype(F32)
    loads[3].wait()
    copies = []
    for piece in range(pieces):
        for plane in range(piece * share, (piece + 1) * share):
            added = source[pl.ds(plane, rows, planes), :]
            result[plane] = advected_ref[plane] + sea * added
        here = pl.ds(piece * share, share)
        copies.append(pltpu.make_async_copy(result.at[here], out_ref.at[here], sem.at[piece]))
        copies[-1].start()
    for copy in copies:
        copy.wait()


def per_device(
    n_lat,
    n_lon,
    atm_fluxes,
    remap_weights,
    source_block,
    target_block,
    block_count,
    tracers,
    east_velocity,
    north_velocity,
    land_mask,
    coupling,
):
    fields, cells = atm_fluxes.shape
    block = remap_weights.shape[-1]
    devices = n_lat * n_lon
    slots = source_block.shape[1] // devices
    tracer_count, levels, rows, cols = tracers.shape
    planes = tracer_count * levels
    groups = tracer_count + 3
    tall = rows + 8
    pairs = planes // 2 + levels
    vmem = pl.BlockSpec(memory_space=pltpu.VMEM)
    anywhere = pl.BlockSpec(memory_space=pl.ANY)
    dma = pltpu.SemaphoreType.DMA
    shape = jax.ShapeDtypeStruct
    flux, advected = pl.pallas_call(
        functools.partial(exchange_kernel, n_lat, n_lon),
        out_shape=(
            shape((rows, fields, block), F32),
            shape((planes, rows, cols), F32),
        ),
        in_specs=[anywhere] * 9,
        out_specs=(vmem, anywhere),
        scratch_shapes=[
            pltpu.SMEM(source_block.shape, jnp.int32),
            pltpu.SMEM(target_block.shape, jnp.int32),
            pltpu.SMEM(block_count.shape, jnp.int32),
            pltpu.VMEM((fields, cells), jnp.bfloat16),
            pltpu.VMEM((rows, cols), jnp.int32),
            pltpu.VMEM((planes, rows, cols), F32),
            pltpu.VMEM((cells // block, fields, block), F32),
            pltpu.VMEM((devices * slots, block, block), jnp.bfloat16),
            pltpu.VMEM((devices, slots * fields, block), F32),
            pltpu.VMEM((devices, slots * fields, block), F32),
            pltpu.VMEM((devices, slots, 1, block), jnp.int32),
            pltpu.VMEM((devices, slots, 1, block), jnp.int32),
            pltpu.VMEM((planes + 2 * levels, tall, cols), F32),
            pltpu.VMEM((tall, cols), F32),
        ]
        + [pltpu.VMEM((pairs + 1, 8, cols), F32)] * 4
        + [pltpu.VMEM((groups, tall, cols), F32)]
        + [pltpu.VMEM((groups // 2 + 1, tall, cols), F32)] * 4
        + [
            pltpu.VMEM((2, groups, tall, cols), F32),
            pltpu.VMEM((NSUB, tracer_count, tall, cols), F32),
            pltpu.VMEM((3, tall, cols), F32),
            dma((8,)),
            dma((devices,)),
            dma((devices,)),
            dma((devices,)),
            dma((devices,)),
            dma((devices,)),
            dma((2,)),
            dma((2,)),
            dma((2,)),
            dma((2,)),
        ],
        compiler_params=pltpu.CompilerParams(
            collective_id=0, has_side_effects=True, vmem_limit_bytes=60 * 1024 * 1024
        ),
    )(
        source_block,
        target_block,
        block_count,
        atm_fluxes,
        remap_weights.reshape(devices * slots, block, block),
        tracers.reshape(planes, rows, cols),
        east_velocity,
        north_velocity,
        land_mask,
    )
    out = pl.pallas_call(
        couple_kernel,
        out_shape=shape((planes, rows, cols), F32),
        in_specs=[anywhere] * 4,
        out_specs=anywhere,
        scratch_shapes=[
            pltpu.VMEM((rows, fields, block), F32),
            pltpu.VMEM((rows, cols), jnp.int32),
            pltpu.VMEM((fields, planes), F32),
            pltpu.VMEM((planes, rows, cols), F32),
            pltpu.VMEM((rows * planes, cols), F32),
            pltpu.VMEM((planes, rows, cols), F32),
            dma((4,)),
            dma((tracer_count,)),
        ],
        compiler_params=pltpu.CompilerParams(vmem_limit_bytes=60 * 1024 * 1024),
    )(flux, land_mask, coupling.T, advected)
    return out.reshape(tracers.shape)


def solution(mesh):
    placed = (
        P(None, ("lat", "lon")),
        P(("lat", "lon"), None, None, None),
        P(("lat", "lon"), None),
        P(("lat", "lon"), None),
        P(("lat", "lon"), None),
        P(None, None, "lat", "lon"),
        P(None, "lat", "lon"),
        P(None, "lat", "lon"),
        P("lat", "lon"),
        P(),
    )
    return jax.shard_map(
        functools.partial(per_device, mesh.shape["lat"], mesh.shape["lon"]),
        mesh=mesh,
        in_specs=placed,
        out_specs=P(None, None, "lat", "lon"),
        check_vma=False,
    )
```
